512 devices in a mesh: blk: 16 (over z_hi, x, core), tm: 32 (over z_lo, y).
Axes of the slice: x: 4, y: 4, z: 16 (z_hi: 2, z_lo: 8; z = z_hi * 8 + z_lo), core: 2. Of those that a mesh axis runs over, the one named last changes fastest.
Arguments:
- waveform: bfloat16 [400, 3, 20480], P('blk', None, 'tm'), may hold values from -600 to 600
- templates: bfloat16 [64, 12, 3, 600], P('blk'), may hold values from -6 to 6
- station_index: int32 [64, 12], P('blk'), may hold values from 0 to 399, as said below
- channel_mask: int32 [64, 12, 3], P('blk'), may hold values from 0 to 1, as said below
Outputs:
- detection: float32 [64, 20480], P('blk', 'tm')
The draws below stay inside these ranges and needn't reach their ends.
Inputs may be any that keep to these rules, and one draw needn't show every extreme that they name: `station_index`: each template names 12 different stations. `channel_mask`: every template station has at least one used component.
All inputs are finite; a program needn't handle non-finite values.
Results may differ from the reference program's by a relative error of at most 0.0003.
Values may be sent and summed in bfloat16 or wider, within the bound.
A program may use at most 192 MiB of HBM per device.

```python
import math
import jax
import jax.numpy as jnp
from jax import lax

STATIONS = 400
CHANNELS = 3
SUBSET = 12
TPL_LEN = 600
TEMPLATES = 64
SAMPLES = 20480


def draw_waveform(key, part):
    key_base = jax.random.fold_in(key, 11)
    key_gain = jax.random.fold_in(key, 12)
    key_time = jax.random.fold_in(key, 13)
    gains = jnp.exp(jax.random.uniform(key_gain, (STATIONS, CHANNELS, 1), jnp.float32, 0.0, math.log(10.0)))
    envelope = jnp.exp(jax.random.uniform(key_time, (1, 1, SAMPLES), jnp.float32, 0.0, math.log(10.0)))
    base_part = jnp.clip(jax.random.normal(key_base, (STATIONS, CHANNELS, SAMPLES), jnp.float32), -6.0, 6.0)
    return (base_part * gains * envelope).astype(jnp.bfloat16)


def draw_station_index(key, part):
    key_score = jax.random.fold_in(key, 31)
    raw_scores = jax.random.randint(key_score, (TEMPLATES, STATIONS), 0, 1 << 20, dtype=jnp.int32)
    distinct = raw_scores * STATIONS + jnp.arange(STATIONS, dtype=jnp.int32)[None, :]
    picked_values, picked = lax.top_k(distinct, SUBSET)
    return picked.astype(jnp.int32)


def draw_channel_mask(key, part):
    key_bits = jax.random.fold_in(key, 21)
    key_keep = jax.random.fold_in(key, 22)
    random_bits = jax.random.randint(key_bits, (TEMPLATES, SUBSET, CHANNELS), 0, 2, dtype=jnp.int32)
    keeper = jax.random.randint(key_keep, (TEMPLATES, SUBSET, 1), 0, CHANNELS, dtype=jnp.int32)
    forced = (jnp.arange(CHANNELS, dtype=jnp.int32)[None, None, :] == keeper).astype(jnp.int32)
    return jnp.maximum(random_bits, forced)


def block_scale(rng, shape, pieces, smallest, largest):
    def one(axis_at, blocks):
        draws = jax.random.uniform(jax.random.fold_in(jax.random.fold_in(rng, 6), axis_at), (blocks,), jnp.float32, smallest / len(pieces), largest / len(pieces))
        return jnp.repeat(jnp.exp(draws), shape[axis_at] // blocks).reshape((-1,) + (1,) * (len(shape) - axis_at - 1))

    factor_of = one(*pieces[0])
    for cut in pieces[1:]:
        factor_of = factor_of * one(*cut)
    return factor_of


def scatter_about(own_key, dims, width, limit, cuts=(), kind=jnp.bfloat16):
    values = width * jax.random.normal(own_key, dims, jnp.float32)
    if cuts:
        values = values * block_scale(own_key, dims, cuts, -0.22, 0.18)
    return jnp.clip(values, -limit, limit).astype(kind)


def setup_inputs(seed: int = 0) -> dict:
    keys = jax.random.split(jax.random.key(seed), 5)
    return {
        "waveform": draw_waveform(jax.random.fold_in(keys[4], 71), 0),
        "templates": scatter_about(keys[1], (TEMPLATES, SUBSET, CHANNELS, TPL_LEN), 1.0, 6.0, ((0, 16),)),
        "station_index": draw_station_index(jax.random.fold_in(keys[4], 71), 0),
        "channel_mask": draw_channel_mask(jax.random.fold_in(keys[4], 71), 0),
    }


floor_share = 0.25
epsilon = 1e-06

def window_energy(padded, tpl_width):
    squared = padded * padded
    return lax.reduce_window(squared, jnp.array(0.0, squared.dtype), lax.add, (1, 1, tpl_width), (1, 1, 1), 'VALID')

def reference(waveform, templates, station_index, channel_mask):
    lag_reach = TPL_LEN - 1
    padded = jnp.concatenate([waveform.astype(jnp.float32), jnp.zeros((STATIONS, CHANNELS, lag_reach), jnp.float32)], axis=2)
    energy = window_energy(padded, TPL_LEN)
    scales = lax.rsqrt(jnp.maximum(energy, floor_share * TPL_LEN))
    shapes_full = templates.astype(jnp.float32)
    template_norm = lax.rsqrt(lax.optimization_barrier(jnp.sum(shapes_full * shapes_full, axis=3)) + epsilon)
    live_mask = channel_mask.astype(jnp.float32)
    counts = lax.optimization_barrier(jnp.sum(live_mask, axis=(1, 2)))
    weights = template_norm * live_mask
    span_len = SAMPLES + lag_reach
    fft_len = 1 << (span_len - 1).bit_length()
    spectra = jnp.fft.rfft(padded, n=fft_len, axis=2)
    members = math.gcd(TEMPLATES, 64)
    blocks = TEMPLATES // members

    def one_block(group_items):
        shapes_block, rows_block, weights_block = group_items
        kernel_spec = jnp.fft.rfft(shapes_block, n=fft_len, axis=3)
        picked = spectra[rows_block]
        correlation = jnp.fft.irfft(picked * jnp.conj(kernel_spec), n=fft_len, axis=3)[..., :SAMPLES]
        window_norms = scales[rows_block]
        return lax.optimization_barrier(jnp.sum(correlation * window_norms * weights_block[..., None], axis=(1, 2)))
    stacked = lax.map(one_block, (shapes_full.reshape(blocks, members, SUBSET, CHANNELS, TPL_LEN), station_index.reshape(blocks, members, SUBSET), weights.reshape(blocks, members, SUBSET, CHANNELS)))
    stacked = stacked.reshape(TEMPLATES, SAMPLES)
    return stacked * jnp.sqrt(TPL_LEN / counts)[:, None]
```

```python
import jax
import jax.numpy as jnp
from jax import lax
from jax.experimental import pallas as pl
from jax.experimental.pallas import tpu as pltpu
from jax.sharding import PartitionSpec as P

bf16, f32, i32 = jnp.bfloat16, jnp.float32, jnp.int32
MESH = pl.DeviceIdType.MESH
NT = (((1,), (1,)), ((), ()))

TPL = 600
TIME = 640
PER = 25
ROWS = 80
SUB = 32
LANES = 128
GROUPS = 36
MEMBERS = 4
TRACES = GROUPS * MEMBERS
STREAMS = 4


def build_toeplitz(t_ref, idx_ref, mask_ref, tz, rid, wcol, mcol, first, last):
    def body(g, carry):
        tt = t_ref[pl.ds(2 * g, 2)].astype(f32).reshape(8, TPL)
        norm = lax.rsqrt(jnp.sum(tt * tt, axis=1, keepdims=True) + 1e-6)
        row0 = pl.multiple_of(8 * g, 8)
        wcol[pl.ds(row0, 8), :] = jnp.broadcast_to(norm, (8, LANES))
        padded = jnp.concatenate([tt, jnp.zeros((8, TIME - TPL), f32)], axis=1)
        for i in range(8):
            jc = 2 * g + i // 4
            k = i % 4
            j = jc // 3
            c = jc - 3 * j
            station = idx_ref[k, j]
            owner = station // PER
            row = owner * ROWS + c * PER + (station - PER * owner)
            rid[pl.ds(row0 + i, 1), :] = jnp.full((1, LANES), row, i32)
            mcol[pl.ds(row0 + i, 1), :] = jnp.full((1, LANES), mask_ref[c, k, j].astype(f32), f32)
            base = jnp.broadcast_to(padded[i : i + 1], (SUB, TIME))
            tz[jc, pl.ds(SUB * k, SUB), :] = pltpu.roll(base, 0, 1, stride=1, stride_axis=0).astype(bf16)
        return carry

    lax.fori_loop(first, last, body, 0)


def band_matrix():
    u = lax.broadcasted_iota(i32, (768, LANES), 0)
    b = lax.broadcasted_iota(i32, (768, LANES), 1)
    d = u - b
    return jnp.where((d >= 0) & (d < TPL), 1.0, 0.0).astype(bf16)


def pick_rows(rid, half, blocks, gain):
    ids = jnp.broadcast_to(rid[:, 0:1], (TRACES, 8 * ROWS))
    number = lax.broadcasted_iota(i32, (TRACES, 8 * ROWS), 1) + half * (8 * ROWS)
    chosen = (jnp.where(ids == number, 1.0, 0.0) * gain).astype(bf16)
    return jnp.dot(chosen, blocks.reshape(8 * ROWS, TIME), preferred_element_type=f32)


def spread(xs, wb):
    full = xs[...]
    for a in range(4):
        moved = full if a == 0 else pltpu.roll(full, 2 * TIME - SUB * a, 1)
        for m in range(10):
            wb[pl.ds(4 * m + a, TRACES, stride=40), :] = moved[:, LANES * m : LANES * (m + 1)]


def window_scales(xs, band, wcol, mcol, sc):
    high, low = [], []
    for m in range(10):
        part = xs[:, LANES * m : LANES * (m + 1)]
        square = part * part
        top = square.astype(bf16)
        high.append(top)
        low.append((square - top.astype(f32)).astype(bf16))
    weight = wcol[...] * mcol[...]
    lane = lax.broadcasted_iota(i32, (TRACES, LANES), 1) // SUB
    member = lax.rem(lax.broadcasted_iota(i32, (TRACES, LANES), 0), MEMBERS)
    for a in range(5):
        energy = jnp.dot(jnp.concatenate(high[a : a + 6], axis=1), band, preferred_element_type=f32)
        energy += jnp.dot(jnp.concatenate(low[a : a + 6], axis=1), band, preferred_element_type=f32)
        scale = lax.rsqrt(jnp.maximum(energy, 0.25 * TPL)) * weight
        turned = [scale] + [pltpu.roll(scale, SUB * d, 1) for d in range(1, 4)]
        for a2 in range(4):
            v = jnp.zeros((TRACES, LANES), f32)
            for k in range(MEMBERS):
                v = jnp.where((lane == k) & (member == k), turned[(k - a2) % 4], v)
            sc[pl.ds(4 * a + a2, TRACES, stride=24), :] = v


def correlate(tz, wb, sc, unroll=6):
    def body(g, acc):
        for q in range(unroll):
            jc = g * unroll + q
            parts = []
            for k in range(MEMBERS):
                row = pl.multiple_of((jc * MEMBERS + k) * 40, 8)
                parts.append(jnp.concatenate([wb[pl.ds(row + 4 * p, 24), :] for p in range(5)], axis=1))
            windows = jnp.concatenate(parts, axis=0).astype(bf16)
            c = lax.dot_general(windows, tz[jc], NT, preferred_element_type=f32)
            acc = acc + c * sc[pl.ds(pl.multiple_of(jc * 96, 8), 96), :]
        return acc

    return lax.fori_loop(0, GROUPS // unroll, body, jnp.zeros((96, LANES), f32))


def finish(acc, mcol, accs, o_ref):
    counts = jnp.sum(mcol[...].reshape(GROUPS, MEMBERS, LANES), axis=0)
    factor = jnp.sqrt(TPL / counts)
    accs[...] = acc
    lane = lax.broadcasted_iota(i32, (8, LANES), 1) // SUB
    for k in range(MEMBERS):
        out = jnp.zeros((8, LANES), f32)
        for q in range(4):
            rows = accs[pl.ds(24 * k + q, 5, stride=4), :]
            rows = jnp.concatenate([rows, jnp.zeros((3, LANES), f32)], axis=0)
            if q != k:
                rows = pltpu.roll(rows, (SUB * (q - k)) % LANES, 1)
            out = jnp.where(lane == q, rows, out)
        for m in range(5):
            o_ref[k : k + 1, LANES * m : LANES * (m + 1)] = out[m : m + 1, :] * factor[k : k + 1, :]


def kernel(
    w_ref, t_ref, idx_ref, mask_ref, o_ref,
    gm, gh, relay, tz, rid, wcol, mcol, xs, wb, sc, accs,
    x_send, x_recv, s_send, s_recv, z_send, z_recv, h_send, h_recv,
):
    blk, tm = lax.axis_index("blk"), lax.axis_index("tm")
    zh, x, core = blk // 8, lax.rem(blk // 2, 4), lax.rem(blk, 2)
    zl, y = tm // 4, lax.rem(tm, 4)
    z = zh * 8 + zl
    turn = 1 - 2 * core

    def at_z(to):
        to = lax.rem(to + 32, 16)
        return (lax.div(to, 8) * 8 + x * 2 + core, lax.rem(to, 8) * 4 + y)

    def at_x(to):
        return (zh * 8 + lax.rem(to + 8, 4) * 2 + core, tm)

    ahead, behind = at_x(x + turn), at_x(x - turn)
    sibling = (zh * 8 + x * 2 + 1 - core, tm)
    z_ahead, z_behind = at_z(z + 4 * turn), at_z(z - 4 * turn)
    later, earlier = (blk, lax.rem(tm + 1, 32)), (blk, lax.rem(tm + 31, 32))

    barrier = pltpu.get_barrier_semaphore()
    friends = (ahead, behind, sibling, z_ahead, z_behind, later, earlier)
    for friend in friends:
        pl.semaphore_signal(barrier, inc=1, device_id=friend, device_id_type=MESH)

    own = w_ref[...].astype(f32)
    packed = jnp.concatenate([own[0], own[1], own[2], jnp.zeros((ROWS - 3 * PER, TIME), f32)], axis=0)
    gm[blk] = packed.astype(bf16)
    pl.semaphore_wait(barrier, len(friends))

    def copy(src, dst, send, recv, to):
        return pltpu.make_async_remote_copy(
            src_ref=src, dst_ref=dst, send_sem=send, recv_sem=recv, device_id=to, device_id_type=MESH
        )

    half = [zh, 1 - zh, zh, 1 - zh]
    store = [gm, gm, gh, gh]
    around = [x, x - turn, x + turn, x + 2]

    def slot(s, place, c):
        return store[s].at[half[s] * 8 + lax.rem(place + 8, 4) * 2 + c]

    def x_copy(s, n):
        block = slot(s, around[1] if n == 2 else around[0], core)
        return copy(block, block, x_send.at[s, n], x_recv.at[s, n], behind if n == 1 else ahead)

    def x_wait(s, n):
        place = (x - turn, x + turn, x + 2)[n]
        block = slot(s, place, core)
        copy(block, block, x_send.at[s, n], x_recv.at[s, n], behind).wait_recv()

    def s_copy(s, n):
        block = slot(s, around[n], core)
        return copy(block, block, s_send.at[s, n], s_recv.at[s, n], sibling)

    def s_wait(s, n):
        place = (x, x + turn, x - turn, x + 2)[n]
        block = slot(s, place, 1 - core)
        copy(block, block, s_send.at[s, n], s_recv.at[s, n], sibling).wait_recv()

    mine, theirs = gm.at[blk], gm.at[(1 - zh) * 8 + x * 2 + core]
    z_first = copy(mine, relay, z_send.at[0], z_recv.at[0], z_ahead)
    z_second = copy(relay, gm.at[lax.rem(lax.div(lax.rem(z - 4 * turn + 32, 16), 8), 2) * 8 + x * 2 + core],
                    z_send.at[1], z_recv.at[1], z_ahead)
    z_arrive = copy(relay, theirs, z_send.at[1], z_recv.at[1], z_behind)
    h_copies = [
        copy(mine, gh.at[blk], h_send.at[0], h_recv.at[0], earlier),
        copy(theirs, gh.at[(1 - zh) * 8 + x * 2 + core], h_send.at[1], h_recv.at[1], earlier),
    ]

    def base_ready(s):
        x_copy(s, 0).start()
        x_copy(s, 1).start()
        s_copy(s, 0).start()

    def from_behind(s):
        x_wait(s, 0)
        x_copy(s, 2).start()
        s_copy(s, 1).start()

    def from_ahead(s):
        x_wait(s, 1)
        s_copy(s, 2).start()

    def far(s):
        x_wait(s, 2)
        s_copy(s, 3).start()

    def build(first, last):
        build_toeplitz(t_ref, idx_ref, mask_ref, tz, rid, wcol, mcol, first, last)

    z_first.start()
    h_copies[0].start()
    base_ready(0)
    build(0, 6)
    from_behind(0)
    from_ahead(0)
    h_copies[0].wait_recv()
    base_ready(2)
    z_first.wait_recv()
    z_second.start()
    build(6, 12)
    far(0)
    from_behind(2)
    from_ahead(2)
    build(12, 18)
    far(2)
    for n in range(4):
        s_wait(0, n)
    z_arrive.wait_recv()
    h_copies[1].start()
    base_ready(1)
    xs[:, :TIME] = pick_rows(rid, zh, gm[pl.ds(zh * 8, 8)], 1.0)
    from_behind(1)
    from_ahead(1)
    h_copies[1].wait_recv()
    base_ready(3)
    for n in range(4):
        s_wait(2, n)
    inside = jnp.where(tm < 31, 1.0, 0.0)
    xs[:, TIME:] = pick_rows(rid, zh, gh[pl.ds(zh * 8, 8)], inside)
    far(1)
    from_behind(3)
    from_ahead(3)
    for n in range(4):
        s_wait(1, n)
    xs[:, :TIME] += pick_rows(rid, 1 - zh, gm[pl.ds((1 - zh) * 8, 8)], 1.0)
    band = band_matrix()
    far(3)
    for n in range(4):
        s_wait(3, n)
    xs[:, TIME:] += pick_rows(rid, 1 - zh, gh[pl.ds((1 - zh) * 8, 8)], inside)

    spread(xs, wb)
    window_scales(xs, band, wcol, mcol, sc)
    finish(correlate(tz, wb, sc), mcol, accs, o_ref)

    z_first.wait_send()
    z_second.wait_send()
    for h in h_copies:
        h.wait_send()
    for s in range(STREAMS):
        for n in range(3):
            x_copy(s, n).wait_send()
        for n in range(4):
            s_copy(s, n).wait_send()


def per_device(waveform, templates, station_index, channel_mask):
    w = jnp.transpose(waveform, (1, 0, 2))
    t = jnp.transpose(templates, (1, 2, 0, 3)).reshape(GROUPS, MEMBERS, TPL)
    mask = jnp.transpose(channel_mask, (2, 0, 1))
    vmem, smem = pl.BlockSpec(memory_space=pltpu.VMEM), pl.BlockSpec(memory_space=pltpu.SMEM)
    dma = pltpu.SemaphoreType.DMA
    return pl.pallas_call(
        kernel,
        out_shape=jax.ShapeDtypeStruct((MEMBERS, TIME), f32),
        in_specs=[vmem, vmem, smem, smem],
        out_specs=vmem,
        scratch_shapes=[
            pltpu.VMEM((16, ROWS, TIME), bf16),
            pltpu.VMEM((16, ROWS, TIME), bf16),
            pltpu.VMEM((ROWS, TIME), bf16),
            pltpu.VMEM((GROUPS, LANES, TIME), bf16),
            pltpu.VMEM((TRACES, LANES), i32),
            pltpu.VMEM((TRACES, LANES), f32),
            pltpu.VMEM((TRACES, LANES), f32),
            pltpu.VMEM((TRACES, 2 * TIME), f32),
            pltpu.VMEM((TRACES * 40, LANES), f32),
            pltpu.VMEM((TRACES * 24, LANES), f32),
            pltpu.VMEM((96, LANES), f32),
            dma((STREAMS, 3)),
            dma((STREAMS, 3)),
            dma((STREAMS, 4)),
            dma((STREAMS, 4)),
            dma((2,)),
            dma((2,)),
            dma((2,)),
            dma((2,)),
        ],
        compiler_params=pltpu.CompilerParams(
            collective_id=0, has_side_effects=True, vmem_limit_bytes=40 * 2**20
        ),
    )(w, t, station_index, mask)


def solution(mesh):
    return jax.shard_map(
        per_device,
        mesh=mesh,
        in_specs=(
            P("blk", None, "tm"),
            P("blk", None, None, None),
            P("blk", None),
            P("blk", None, None),
        ),
        out_specs=P("blk", "tm"),
        check_vma=False,
    )
```

```python
import jax
import jax.numpy as jnp
from jax import lax
from jax.experimental import pallas as pl
from jax.experimental.pallas import tpu as pltpu
from jax.sharding import PartitionSpec as P

bf16, f32, i32 = jnp.bfloat16, jnp.float32, jnp.int32
MESH = pl.DeviceIdType.MESH
NT = (((1,), (1,)), ((), ()))

TPL = 600
TIME = 640
PER = 25
ROWS = 80
SUB = 32
LANES = 128
GROUPS = 36
MEMBERS = 4
TRACES = GROUPS * MEMBERS
HALF = 8 * ROWS
SLOTS = 8
QUARTER = GROUPS // 4


def build_toeplitz(t_ref, tz, wcol, base):
    def body(g, carry):
        tt = t_ref[pl.ds(2 * g, 2)].astype(f32).reshape(8, TPL)
        norm = lax.rsqrt(jnp.sum(tt * tt, axis=1, keepdims=True) + 1e-6)
        wcol[pl.ds(pl.multiple_of(base + 8 * g, 8), 8), :] = jnp.broadcast_to(norm, (8, LANES))
        padded = jnp.concatenate([tt, jnp.zeros((8, TIME - TPL), f32)], axis=1)
        for i in range(8):
            rows = jnp.broadcast_to(padded[i : i + 1], (SUB, TIME))
            tz[2 * g + i // 4, pl.ds(SUB * (i % 4), SUB), :] = pltpu.roll(
                rows, 0, 1, stride=1, stride_axis=0
            ).astype(bf16)
        return carry

    lax.fori_loop(0, GROUPS // 2, body, 0)


def number_rows(idx_ref, mask_ref, zh, mine, theirs, mcol):
    def body(g, carry):
        row0 = pl.multiple_of(8 * g, 8)
        for i in range(8):
            jc = 2 * g + i // 4
            k = i % 4
            j = jc // 3
            c = jc - 3 * j
            station = idx_ref[k, j]
            used = mask_ref[c, k, j]
            owner = station // PER
            half = owner // 8
            row = ((owner - 8 * half) * ROWS + c * PER + (station - PER * owner) + 1) * used
            here = half * zh + (1 - half) * (1 - zh)
            mine[pl.ds(row0 + i, 1), :] = jnp.full((1, LANES), (row * here).astype(f32), f32)
            theirs[pl.ds(row0 + i, 1), :] = jnp.full((1, LANES), (row * (1 - here)).astype(f32), f32)
            mcol[pl.ds(row0 + i, 1), :] = jnp.full((1, LANES), used.astype(f32), f32)
        return carry

    lax.fori_loop(0, GROUPS // 2, body, 0)


def band_matrix():
    u = lax.broadcasted_iota(i32, (768, LANES), 0)
    b = lax.broadcasted_iota(i32, (768, LANES), 1)
    d = u - b
    return jnp.where((d >= 0) & (d < TPL), 1.0, 0.0).astype(bf16)


def choose(rows, ids, base):
    number = lax.broadcasted_iota(i32, (TRACES, HALF), 1).astype(f32) + 1.0
    ids[pl.ds(base, TRACES), :] = jnp.where(jnp.broadcast_to(rows, (TRACES, HALF)) == number, 1.0, 0.0).astype(bf16)


def pick(ids, store, first, count):
    blocks = [store[:, first + i].reshape(HALF, LANES) for i in range(count)]
    return jnp.dot(ids, jnp.concatenate(blocks, axis=1), preferred_element_type=f32)


def spread(xs, wb, base):
    full = xs[pl.ds(base, TRACES), :]
    for a in range(4):
        moved = full if a == 0 else pltpu.roll(full, 2 * TIME - SUB * a, 1)
        for m in range(10):
            wb[pl.ds(40 * base + 4 * m + a, TRACES, stride=40), :] = moved[:, LANES * m : LANES * (m + 1)]


def window_scales(xs, band, sc, base):
    high, low = [], []
    for m in range(10):
        part = xs[pl.ds(base, TRACES), LANES * m : LANES * (m + 1)]
        square = part * part
        top = square.astype(bf16)
        high.append(top)
        low.append((square - top.astype(f32)).astype(bf16))
    lane = lax.broadcasted_iota(i32, (TRACES, LANES), 1) // SUB
    member = lax.rem(lax.broadcasted_iota(i32, (TRACES, LANES), 0), MEMBERS)
    for a in range(5):
        energy = jnp.dot(jnp.concatenate(high[a : a + 6], axis=1), band, preferred_element_type=f32)
        energy += jnp.dot(jnp.concatenate(low[a : a + 6], axis=1), band, preferred_element_type=f32)
        scale = lax.rsqrt(jnp.maximum(energy, 0.25 * TPL))
        turned = [scale] + [pltpu.roll(scale, SUB * d, 1) for d in range(1, 4)]
        for a2 in range(4):
            v = jnp.zeros((TRACES, LANES), f32)
            for k in range(MEMBERS):
                v = jnp.where((lane == k) & (member == k), turned[(k - a2) % 4], v)
            sc[pl.ds(24 * base + 4 * a + a2, TRACES, stride=24), :] = v


def correlate(tz, wb, sc, wcol, base, unroll=6):
    def body(g, acc):
        for q in range(unroll):
            jc = g * unroll + q
            parts, gains = [], []
            for k in range(MEMBERS):
                trace = base + jc * MEMBERS + k
                row = pl.multiple_of(trace * 40, 8)
                parts.append(jnp.concatenate([wb[pl.ds(row + 4 * p, 24), :] for p in range(5)], axis=1))
                gains.append(jnp.broadcast_to(wcol[pl.ds(trace, 1), :], (24, LANES)))
            windows = jnp.concatenate(parts, axis=0).astype(bf16)
            c = lax.dot_general(windows, tz[jc], NT, preferred_element_type=f32)
            scale = sc[pl.ds(pl.multiple_of((base + jc * MEMBERS) * 24, 8), 96), :]
            acc = acc + c * (scale * jnp.concatenate(gains, axis=0))
        return acc

    acc = lax.fori_loop(0, GROUPS // unroll, body, jnp.zeros((96, LANES), f32))
    return (acc[0:24] + acc[24:48]) + (acc[48:72] + acc[72:96])


def finish(sums, mcol, o_ref):
    counts = jnp.sum(mcol[...].reshape(GROUPS, MEMBERS, LANES), axis=0)
    factor = jnp.sqrt(TPL / counts)
    lane = lax.broadcasted_iota(i32, (8, LANES), 1) // SUB
    quads = [sums[pl.ds(q, 5, stride=4), :] for q in range(4)]
    quads = [jnp.concatenate([rows, jnp.zeros((3, LANES), f32)], axis=0) for rows in quads]
    for k in range(MEMBERS):
        out = jnp.zeros((8, LANES), f32)
        for q in range(4):
            rows = quads[q] if q == k else pltpu.roll(quads[q], (SUB * (q - k)) % LANES, 1)
            out = jnp.where(lane == q, rows, out)
        for m in range(5):
            o_ref[k : k + 1, LANES * m : LANES * (m + 1)] = out[m : m + 1, :] * factor[k : k + 1, :]


def kernel(
    w_hbm, t_hbm, idx_hbm, mask_hbm, o_ref,
    w_ref, t_ref, idx_ref, mask_ref, t_far, n_out, n_in, gm, gh, ids, tz, tz_far, mine, theirs, wcol, mcol,
    xs, wb, sc, r_out, r_in, sums,
    in_sem, x_send, x_recv, s_send, s_recv, h_send, h_recv, t_send, t_recv, y_send, y_recv, n_send, n_recv, r_send, r_recv,
):
    blk, tm = lax.axis_index("blk"), lax.axis_index("tm")
    zh, x, core = blk // 8, lax.rem(blk // 2, 4), lax.rem(blk, 2)
    zl, y = tm // 4, lax.rem(tm, 4)

    def at(place, c):
        return lax.rem(place + 4, 4) * 2 + c

    loads = [
        pltpu.make_async_copy(src, dst, in_sem.at[i])
        for i, (src, dst) in enumerate(
            ((w_hbm, w_ref), (idx_hbm, idx_ref), (mask_hbm, mask_ref), (t_hbm, t_ref))
        )
    ]
    for load in loads:
        load.start()

    other = (1 - zh) * 8 + at(x, core)
    partner = (other, tm)
    mirror = (other, (7 - zl) * 4 + y)
    sibling = (zh * 8 + at(x, 1 - core), tm)
    across = [(zh * 8 + at(x + d, core), tm) for d in (1, -1, 2)]
    column = [(blk, zl * 4 + lax.rem(y + d + 4, 4)) for d in (1, -1, 2)]
    earlier, later = (blk, lax.rem(tm + 31, 32)), (blk, lax.rem(tm + 1, 32))
    has_earlier, has_later = tm > 0, tm < 31

    barrier = pltpu.get_barrier_semaphore()
    friends = (mirror, partner, *across, *column, sibling)
    for friend in friends:
        pl.semaphore_signal(barrier, inc=1, device_id=friend, device_id_type=MESH)

    @pl.when(has_earlier)
    def _():
        pl.semaphore_signal(barrier, inc=1, device_id=earlier, device_id_type=MESH)

    @pl.when(has_later)
    def _():
        pl.semaphore_signal(barrier, inc=1, device_id=later, device_id_type=MESH)

    loads[0].wait()
    own = w_ref[...].astype(f32)
    packed = jnp.concatenate([own[0], own[1], own[2], jnp.zeros((ROWS - 3 * PER, TIME), f32)], axis=0)
    slot = at(x, core)
    for m in range(5):
        gm[slot, m] = packed[:, LANES * m : LANES * (m + 1)].astype(bf16)
    pl.semaphore_wait(barrier, len(friends) + has_earlier.astype(i32) + has_later.astype(i32))

    def copy(src, dst, send, recv, to):
        return pltpu.make_async_remote_copy(
            src_ref=src, dst_ref=dst, send_sem=send, recv_sem=recv, device_id=to, device_id_type=MESH
        )

    store = (gm, gh)

    def x_copy(s, n):
        block = store[s].at[slot]
        return copy(block, block, x_send.at[s, n], x_recv.at[s, n], across[n])

    def x_wait(s, n):
        block = store[s].at[at(x + (-1, 1, 2)[n], core)]
        copy(block, block, x_send.at[s, n], x_recv.at[s, n], across[n]).wait_recv()

    def s_copy(s, n):
        block = store[s].at[at(x + (0, -1, 1, 2)[n], core)]
        return copy(block, block, s_send.at[s, n], s_recv.at[s, n], sibling)

    def s_wait(s):
        for n in range(4):
            block = store[s].at[at(x + (0, -1, 1, 2)[n], 1 - core)]
            copy(block, block, s_send.at[s, n], s_recv.at[s, n], sibling).wait_recv()

    h_copy = copy(gm.at[slot], gh.at[slot], h_send, h_recv, earlier)

    def quarter(ref, part):
        return ref.at[pl.ds(QUARTER * lax.rem(part + 4, 4), QUARTER)]

    t_copy = copy(quarter(t_hbm, y), quarter(t_far, y), t_send, t_recv, mirror)

    def y_copy(n):
        block = quarter(t_far, y)
        return copy(block, block, y_send.at[n], y_recv.at[n], column[n])

    def y_wait(n):
        block = quarter(t_far, y + (-1, 1, 2)[n])
        copy(block, block, y_send.at[n], y_recv.at[n], column[n]).wait_recv()

    n_copy = copy(n_out, n_in, n_send, n_recv, mirror)
    r_copy = copy(r_out, r_in, r_send, r_recv, partner)

    def fan(s):
        for n in range(3):
            x_copy(s, n).start()
        s_copy(s, 0).start()

    def hand_over(s):
        for n in range(3):
            x_wait(s, n)
            s_copy(s, 1 + n).start()

    t_copy.start()

    @pl.when(has_earlier)
    def _():
        h_copy.start()

    fan(0)
    loads[1].wait()
    loads[2].wait()
    number_rows(idx_ref, mask_ref, zh, mine, theirs, mcol)
    flat = jnp.transpose(theirs[...])[0:8, :]
    sixteens = jnp.floor(flat * (1.0 / 16.0))
    n_out[...] = jnp.concatenate([sixteens, flat - 16.0 * sixteens], axis=0).astype(bf16)
    n_copy.start()
    loads[3].wait()
    choose(mine[0:TRACES, 0:1], ids, 0)

    @pl.when(has_later)
    def _():
        h_copy.wait_recv()

    @pl.when(jnp.logical_not(has_later))
    def _():
        for m in range(5):
            gh[slot, m] = jnp.zeros((ROWS, LANES), bf16)

    fan(1)
    hand_over(0)
    build_toeplitz(t_ref, tz, wcol, 0)
    n_copy.wait_recv()
    got = n_in[...].astype(f32)
    choose(jnp.transpose(got[0:8] * 16.0 + got[8:16])[0:TRACES, 0:1], ids, TRACES)
    t_copy.wait_recv()
    for n in range(3):
        y_copy(n).start()
    s_wait(0)
    xs[:, :TIME] = pick(ids[...], gm, 0, 5)
    hand_over(1)
    s_wait(1)
    xs[:, TIME:] = pick(ids[...], gh, 0, 5)
    band = band_matrix()
    for base in (TRACES, 0):
        spread(xs, wb, base)
        window_scales(xs, band, sc, base)
    for n in range(3):
        y_wait(n)
    build_toeplitz(t_far, tz_far, wcol, TRACES)
    r_out[...] = correlate(tz_far, wb, sc, wcol, TRACES)
    r_copy.start()
    total = correlate(tz, wb, sc, wcol, 0)
    r_copy.wait_recv()
    sums[...] = total + r_in[...]
    finish(sums, mcol, o_ref)

    for n in range(3):
        y_copy(n).wait_send()
        for s in range(2):
            x_copy(s, n).wait_send()
    for n in range(4):
        for s in range(2):
            s_copy(s, n).wait_send()
    for sent in (t_copy, n_copy, r_copy):
        sent.wait_send()

    @pl.when(has_earlier)
    def _():
        h_copy.wait_send()


def per_device(waveform, templates, station_index, channel_mask):
    w = jnp.transpose(waveform, (1, 0, 2))
    t = jnp.transpose(templates, (1, 2, 0, 3)).reshape(GROUPS, MEMBERS, TPL)
    mask = jnp.transpose(channel_mask, (2, 0, 1))
    anywhere = pl.BlockSpec(memory_space=pl.ANY)
    dma = pltpu.SemaphoreType.DMA
    return pl.pallas_call(
        kernel,
        out_shape=jax.ShapeDtypeStruct((MEMBERS, TIME), f32),
        in_specs=[anywhere] * 4,
        out_specs=pl.BlockSpec(memory_space=pltpu.VMEM),
        scratch_shapes=[
            pltpu.VMEM(w.shape, bf16),
            pltpu.VMEM(t.shape, bf16),
            pltpu.SMEM(station_index.shape, i32),
            pltpu.SMEM(mask.shape, i32),
            pltpu.VMEM(t.shape, bf16),
            pltpu.VMEM((16, 256), bf16),
            pltpu.VMEM((16, 256), bf16),
            pltpu.VMEM((SLOTS, 5, ROWS, LANES), bf16),
            pltpu.VMEM((SLOTS, 5, ROWS, LANES), bf16),
            pltpu.VMEM((2 * TRACES, HALF), bf16),
            pltpu.VMEM((GROUPS, LANES, TIME), bf16),
            pltpu.VMEM((GROUPS, LANES, TIME), bf16),
            pltpu.VMEM((256, LANES), f32),
            pltpu.VMEM((256, LANES), f32),
            pltpu.VMEM((2 * TRACES, LANES), f32),
            pltpu.VMEM((TRACES, LANES), f32),
            pltpu.VMEM((2 * TRACES, 2 * TIME), f32),
            pltpu.VMEM((2 * TRACES * 40, LANES), f32),
            pltpu.VMEM((2 * TRACES * 24, LANES), f32),
            pltpu.VMEM((24, LANES), f32),
            pltpu.VMEM((24, LANES), f32),
            pltpu.VMEM((24, LANES), f32),
            dma((4,)),
            dma((2, 3)),
            dma((2, 3)),
            dma((2, 4)),
            dma((2, 4)),
            dma,
            dma,
            dma,
            dma,
            dma((3,)),
            dma((3,)),
            dma,
            dma,
            dma,
            dma,
        ],
        compiler_params=pltpu.CompilerParams(
            collective_id=0, has_side_effects=True, vmem_limit_bytes=56 * 2**20
        ),
    )(w, t, station_index, mask)


def solution(mesh):
    return jax.shard_map(
        per_device,
        mesh=mesh,
        in_specs=(
            P("blk", None, "tm"),
            P("blk", None, None, None),
            P("blk", None),
            P("blk", None, None),
        ),
        out_specs=P("blk", "tm"),
        check_vma=False,
    )
```

```python
import jax
import jax.numpy as jnp
from jax import lax
from jax.experimental import pallas as pl
from jax.experimental.pallas import tpu as pltpu
from jax.sharding import PartitionSpec as P

bf16, f32, i32 = jnp.bfloat16, jnp.float32, jnp.int32
MESH = pl.DeviceIdType.MESH
NT = (((1,), (1,)), ((), ()))

TPL = 600
TIME = 640
PER = 25
ROWS = 80
SUB = 32
LANES = 128
GROUPS = 36
MEMBERS = 4
TRACES = GROUPS * MEMBERS
HALF = 8 * ROWS
SLOTS = 8
QUARTER = GROUPS // 4


def build_toeplitz(t_ref, tz, wcol, first, count, step=3):
    def body(g, carry):
        group = first + step * g
        tt = t_ref[pl.ds(group, step)].astype(f32)
        norm = lax.rsqrt(jnp.sum(tt * tt, axis=2, keepdims=True) + 1e-6)
        wcol[pl.ds(group, step)] = jnp.broadcast_to(norm, (step, MEMBERS, LANES))
        padded = jnp.concatenate([tt, jnp.zeros((step, MEMBERS, TIME - TPL), f32)], axis=2)
        for i in range(step):
            for k in range(MEMBERS):
                rows = jnp.broadcast_to(padded[i, k : k + 1], (SUB, TIME))
                tz[group + i, pl.ds(SUB * k, SUB), :] = pltpu.roll(rows, 0, 1, stride=1, stride_axis=0).astype(bf16)
        return carry

    lax.fori_loop(0, count // step, body, 0)


def number_rows(idx_ref, mask_ref, zh, mine, theirs, mcol):
    def body(g, carry):
        row0 = pl.multiple_of(8 * g, 8)
        for i in range(8):
            jc = 2 * g + i // 4
            k = i % 4
            j = jc // 3
            c = jc - 3 * j
            station = idx_ref[k, j]
            used = mask_ref[c, k, j]
            owner = station // PER
            half = owner // 8
            row = ((owner - 8 * half) * ROWS + c * PER + (station - PER * owner) + 1) * used
            here = half * zh + (1 - half) * (1 - zh)
            mine[pl.ds(row0 + i, 1), :] = jnp.full((1, LANES), (row * here).astype(f32), f32)
            theirs[pl.ds(row0 + i, 1), :] = jnp.full((1, LANES), (row * (1 - here)).astype(f32), f32)
            mcol[pl.ds(row0 + i, 1), :] = jnp.full((1, LANES), used.astype(f32), f32)
        return carry

    lax.fori_loop(0, GROUPS // 2, body, 0)


def band_matrix():
    u = lax.broadcasted_iota(i32, (768, LANES), 0)
    b = lax.broadcasted_iota(i32, (768, LANES), 1)
    d = u - b
    return jnp.where((d >= 0) & (d < TPL), 1.0, 0.0).astype(bf16)


def choose(rows, ids, base):
    number = lax.broadcasted_iota(i32, (TRACES, HALF), 1).astype(f32) + 1.0
    ids[pl.ds(base, TRACES), :] = jnp.where(jnp.broadcast_to(rows, (TRACES, HALF)) == number, 1.0, 0.0).astype(bf16)


def pick(ids, store, first, count):
    blocks = [store[:, first + i].reshape(HALF, LANES) for i in range(count)]
    return jnp.dot(ids, jnp.concatenate(blocks, axis=1), preferred_element_type=f32)


def spread(xs, wb, base):
    full = xs[pl.ds(base, TRACES), :]
    for a in range(4):
        moved = full if a == 0 else pltpu.roll(full, 2 * TIME - SUB * a, 1)
        for m in range(10):
            wb[pl.ds(40 * base + 4 * m + a, TRACES, stride=40), :] = moved[:, LANES * m : LANES * (m + 1)]


def window_scales(xs, band, sc, base):
    high, low = [], []
    for m in range(10):
        part = xs[pl.ds(base, TRACES), LANES * m : LANES * (m + 1)]
        square = part * part
        top = square.astype(bf16)
        high.append(top)
        low.append((square - top.astype(f32)).astype(bf16))
    lane = lax.broadcasted_iota(i32, (TRACES, LANES), 1) // SUB
    member = lax.rem(lax.broadcasted_iota(i32, (TRACES, LANES), 0), MEMBERS)
    for a in range(5):
        energy = jnp.dot(jnp.concatenate(high[a : a + 6], axis=1), band, preferred_element_type=f32)
        energy += jnp.dot(jnp.concatenate(low[a : a + 6], axis=1), band, preferred_element_type=f32)
        scale = lax.rsqrt(jnp.maximum(energy, 0.25 * TPL))
        turned = [scale] + [pltpu.roll(scale, SUB * d, 1) for d in range(1, 4)]
        for a2 in range(4):
            v = jnp.zeros((TRACES, LANES), f32)
            for k in range(MEMBERS):
                v = jnp.where((lane == k) & (member == k), turned[(k - a2) % 4], v)
            sc[pl.ds(24 * base + 4 * a + a2, TRACES, stride=24), :] = v


def correlate(tz, wb, sc, wcol, base, first, count, acc, unroll=9):
    def body(g, acc):
        for q in range(unroll):
            jc = first + g * unroll + q
            parts, gains = [], []
            for k in range(MEMBERS):
                row = pl.multiple_of((base + jc * MEMBERS + k) * 40, 8)
                parts.append(jnp.concatenate([wb[pl.ds(row + 4 * p, 24), :] for p in range(5)], axis=1))
                gains.append(jnp.broadcast_to(wcol[jc, k : k + 1, :], (24, LANES)))
            windows = jnp.concatenate(parts, axis=0).astype(bf16)
            c = lax.dot_general(windows, tz[jc], NT, preferred_element_type=f32)
            scale = sc[pl.ds(pl.multiple_of((base + jc * MEMBERS) * 24, 8), 96), :]
            acc = acc + c * (scale * jnp.concatenate(gains, axis=0))
        return acc

    return lax.fori_loop(0, count // unroll, body, acc)


def fold(acc):
    return (acc[0:24] + acc[24:48]) + (acc[48:72] + acc[72:96])


def finish(sums, mcol, o_ref):
    counts = jnp.sum(mcol[...].reshape(GROUPS, MEMBERS, LANES), axis=0)
    factor = jnp.sqrt(TPL / counts)
    lane = lax.broadcasted_iota(i32, (8, LANES), 1) // SUB
    quads = [sums[pl.ds(q, 5, stride=4), :] for q in range(4)]
    quads = [jnp.concatenate([rows, jnp.zeros((3, LANES), f32)], axis=0) for rows in quads]
    for k in range(MEMBERS):
        out = jnp.zeros((8, LANES), f32)
        for q in range(4):
            rows = quads[q] if q == k else pltpu.roll(quads[q], (SUB * (q - k)) % LANES, 1)
            out = jnp.where(lane == q, rows, out)
        for m in range(5):
            o_ref[k : k + 1, LANES * m : LANES * (m + 1)] = out[m : m + 1, :] * factor[k : k + 1, :]


def kernel(
    w_hbm, t_hbm, idx_hbm, mask_hbm, o_ref,
    w_ref, t_ref, idx_ref, mask_ref, t_far, n_out, n_in, gm, gh, ids, tz, tz_far, mine, theirs, wcol, wcol_far, mcol,
    xs, wb, sc, r_out, r_in, sums,
    in_sem, x_send, x_recv, s_send, s_recv, h_send, h_recv, t_send, t_recv, y_send, y_recv, n_send, n_recv, r_send, r_recv,
):
    blk, tm = lax.axis_index("blk"), lax.axis_index("tm")
    zh, x, core = blk // 8, lax.rem(blk // 2, 4), lax.rem(blk, 2)
    zl, y = tm // 4, lax.rem(tm, 4)

    def at(place, c):
        return lax.rem(place + 4, 4) * 2 + c

    loads = [
        pltpu.make_async_copy(src, dst, in_sem.at[i])
        for i, (src, dst) in enumerate(
            ((w_hbm, w_ref), (idx_hbm, idx_ref), (mask_hbm, mask_ref), (t_hbm, t_ref))
        )
    ]
    for load in loads:
        load.start()

    other = (1 - zh) * 8 + at(x, core)
    partner = (other, tm)
    mirror = (other, (7 - zl) * 4 + y)
    sibling = (zh * 8 + at(x, 1 - core), tm)
    across = [(zh * 8 + at(x + d, core), tm) for d in (1, -1, 2)]
    column = [(blk, zl * 4 + lax.rem(y + d + 4, 4)) for d in (1, -1, 2)]
    earlier, later = (blk, lax.rem(tm + 31, 32)), (blk, lax.rem(tm + 1, 32))
    has_earlier, has_later = tm > 0, tm < 31

    barrier = pltpu.get_barrier_semaphore()
    friends = (mirror, partner, *across, *column, sibling)
    for friend in friends:
        pl.semaphore_signal(barrier, inc=1, device_id=friend, device_id_type=MESH)

    @pl.when(has_earlier)
    def _():
        pl.semaphore_signal(barrier, inc=1, device_id=earlier, device_id_type=MESH)

    @pl.when(has_later)
    def _():
        pl.semaphore_signal(barrier, inc=1, device_id=later, device_id_type=MESH)

    loads[0].wait()
    own = w_ref[...].astype(f32)
    packed = jnp.concatenate([own[0], own[1], own[2], jnp.zeros((ROWS - 3 * PER, TIME), f32)], axis=0)
    slot = at(x, core)
    for m in range(5):
        gm[slot, m] = packed[:, LANES * m : LANES * (m + 1)].astype(bf16)
    loads[3].wait()
    build_toeplitz(t_ref, tz, wcol, 0, GROUPS)
    pl.semaphore_wait(barrier, len(friends) + has_earlier.astype(i32) + has_later.astype(i32))

    def copy(src, dst, send, recv, to):
        return pltpu.make_async_remote_copy(
            src_ref=src, dst_ref=dst, send_sem=send, recv_sem=recv, device_id=to, device_id_type=MESH
        )

    store = (gm, gh)

    def x_copy(s, n):
        block = store[s].at[slot]
        return copy(block, block, x_send.at[s, n], x_recv.at[s, n], across[n])

    def x_wait(s, n):
        block = store[s].at[at(x + (-1, 1, 2)[n], core)]
        copy(block, block, x_send.at[s, n], x_recv.at[s, n], across[n]).wait_recv()

    def s_copy(s, n):
        block = store[s].at[at(x + (0, -1, 1, 2)[n], core)]
        return copy(block, block, s_send.at[s, n], s_recv.at[s, n], sibling)

    def s_wait(s):
        for n in range(4):
            block = store[s].at[at(x + (0, -1, 1, 2)[n], 1 - core)]
            copy(block, block, s_send.at[s, n], s_recv.at[s, n], sibling).wait_recv()

    facing = at(x + 2, core)
    h_copies = [
        copy(gm.at[place], gh.at[place], h_send.at[n], h_recv.at[n], earlier) for n, place in enumerate((slot, facing))
    ]

    def h_start(n):
        @pl.when(has_earlier)
        def _():
            h_copies[n].start()

    def h_wait(n):
        @pl.when(has_later)
        def _():
            h_copies[n].wait_recv()

        @pl.when(jnp.logical_not(has_later))
        def _():
            for m in range(5):
                gh[(slot, facing)[n], m] = jnp.zeros((ROWS, LANES), bf16)


    def quarter(ref, part):
        return ref.at[pl.ds(QUARTER * lax.rem(part + 4, 4), QUARTER)]

    t_copy = copy(quarter(t_hbm, y), quarter(t_far, y), t_send, t_recv, mirror)

    def y_copy(n):
        block = quarter(t_far, y)
        return copy(block, block, y_send.at[n], y_recv.at[n], column[n])

    def y_wait(n):
        block = quarter(t_far, y + (-1, 1, 2)[n])
        copy(block, block, y_send.at[n], y_recv.at[n], column[n]).wait_recv()

    n_copy = copy(n_out, n_in, n_send, n_recv, mirror)
    r_copy = copy(r_out, r_in, r_send, r_recv, partner)

    t_copy.start()
    h_start(0)
    for n in range(3):
        x_copy(0, n).start()
    s_copy(0, 0).start()
    loads[1].wait()
    loads[2].wait()
    number_rows(idx_ref, mask_ref, zh, mine, theirs, mcol)
    flat = jnp.transpose(theirs[...])[0:8, :]
    sixteens = jnp.floor(flat * (1.0 / 16.0))
    n_out[...] = jnp.concatenate([sixteens, flat - 16.0 * sixteens], axis=0).astype(bf16)
    n_copy.start()
    choose(mine[0:TRACES, 0:1], ids, 0)
    h_wait(0)
    for n in range(2):
        x_copy(1, n).start()
    s_copy(1, 0).start()
    x_wait(0, 2)
    h_start(1)
    s_copy(0, 3).start()
    t_copy.wait_recv()
    for n in range(3):
        y_copy(n).start()
    for n in range(2):
        x_wait(0, n)
        s_copy(0, 1 + n).start()
    build_toeplitz(t_far, tz_far, wcol_far, QUARTER * y, QUARTER)
    n_copy.wait_recv()
    got = n_in[...].astype(f32)
    choose(jnp.transpose(got[0:8] * 16.0 + got[8:16])[0:TRACES, 0:1], ids, TRACES)
    h_wait(1)
    s_copy(1, 3).start()
    for n in range(2):
        x_wait(1, n)
        s_copy(1, 1 + n).start()
    s_wait(0)
    xs[:, :TIME] = pick(ids[...], gm, 0, 5)
    band = band_matrix()
    for n in range(3):
        y_wait(n)
        build_toeplitz(t_far, tz_far, wcol_far, QUARTER * lax.rem(y + (3, 1, 2)[n], 4), QUARTER)
    s_wait(1)
    xs[:, TIME:] = pick(ids[...], gh, 0, 5)
    spread(xs, wb, TRACES)
    window_scales(xs, band, sc, TRACES)
    acc = jnp.zeros((96, LANES), f32)
    acc = correlate(tz_far, wb, sc, wcol_far, TRACES, 0, GROUPS, acc, 12)
    r_out[...] = fold(acc)
    r_copy.start()
    spread(xs, wb, 0)
    window_scales(xs, band, sc, 0)
    total = fold(correlate(tz, wb, sc, wcol, 0, 0, GROUPS, jnp.zeros((96, LANES), f32), 12))
    r_copy.wait_recv()
    sums[...] = total + r_in[...]
    finish(sums, mcol, o_ref)

    for n in range(3):
        y_copy(n).wait_send()
        x_copy(0, n).wait_send()
    for n in range(2):
        x_copy(1, n).wait_send()
    for n in range(4):
        for s in range(2):
            s_copy(s, n).wait_send()
    for sent in (t_copy, n_copy, r_copy):
        sent.wait_send()

    @pl.when(has_earlier)
    def _():
        for h in h_copies:
            h.wait_send()


def per_device(waveform, templates, station_index, channel_mask):
    w = jnp.transpose(waveform, (1, 0, 2))
    t = jnp.transpose(templates, (1, 2, 0, 3)).reshape(GROUPS, MEMBERS, TPL)
    mask = jnp.transpose(channel_mask, (2, 0, 1))
    anywhere = pl.BlockSpec(memory_space=pl.ANY)
    dma = pltpu.SemaphoreType.DMA
    return pl.pallas_call(
        kernel,
        out_shape=jax.ShapeDtypeStruct((MEMBERS, TIME), f32),
        in_specs=[anywhere] * 4,
        out_specs=pl.BlockSpec(memory_space=pltpu.VMEM),
        scratch_shapes=[
            pltpu.VMEM(w.shape, bf16),
            pltpu.VMEM(t.shape, bf16),
            pltpu.SMEM(station_index.shape, i32),
            pltpu.SMEM(mask.shape, i32),
            pltpu.VMEM(t.shape, bf16),
            pltpu.VMEM((16, 256), bf16),
            pltpu.VMEM((16, 256), bf16),
            pltpu.VMEM((SLOTS, 5, ROWS, LANES), bf16),
            pltpu.VMEM((SLOTS, 5, ROWS, LANES), bf16),
            pltpu.VMEM((2 * TRACES, HALF), bf16),
            pltpu.VMEM((GROUPS, LANES, TIME), bf16),
            pltpu.VMEM((GROUPS, LANES, TIME), bf16),
            pltpu.VMEM((256, LANES), f32),
            pltpu.VMEM((256, LANES), f32),
            pltpu.VMEM((GROUPS, MEMBERS, LANES), f32),
            pltpu.VMEM((GROUPS, MEMBERS, LANES), f32),
            pltpu.VMEM((TRACES, LANES), f32),
            pltpu.VMEM((2 * TRACES, 2 * TIME), f32),
            pltpu.VMEM((2 * TRACES * 40, LANES), f32),
            pltpu.VMEM((2 * TRACES * 24, LANES), f32),
            pltpu.VMEM((24, LANES), f32),
            pltpu.VMEM((24, LANES), f32),
            pltpu.VMEM((24, LANES), f32),
            dma((4,)),
            dma((2, 3)),
            dma((2, 3)),
            dma((2, 4)),
            dma((2, 4)),
            dma((2,)),
            dma((2,)),
            dma,
            dma,
            dma((3,)),
            dma((3,)),
            dma,
            dma,
            dma,
            dma,
        ],
        compiler_params=pltpu.CompilerParams(
            collective_id=0, has_side_effects=True, vmem_limit_bytes=56 * 2**20
        ),
    )(w, t, station_index, mask)


def solution(mesh):
    return jax.shard_map(
        per_device,
        mesh=mesh,
        in_specs=(
            P("blk", None, "tm"),
            P("blk", None, None, None),
            P("blk", None),
            P("blk", None, None),
        ),
        out_specs=P("blk", "tm"),
        check_vma=False,
    )
```

```python
import jax
import jax.numpy as jnp
from jax import lax
from jax.experimental import pallas as pl
from jax.experimental.pallas import tpu as pltpu
from jax.sharding import PartitionSpec as P

bf16, f32, i32 = jnp.bfloat16, jnp.float32, jnp.int32
MESH = pl.DeviceIdType.MESH
NT = (((1,), (1,)), ((), ()))

TPL = 600
TIME = 640
PER = 25
ROWS = 80
SUB = 32
LANES = 128
GROUPS = 36
MEMBERS = 4
TRACES = GROUPS * MEMBERS
HALF = 8 * ROWS
SLOTS = 8
QUARTER = GROUPS // 4


def build_toeplitz(t_ref, tz, wcol, first, count, step=3):
    def body(g, carry):
        group = first + step * g
        tt = t_ref[pl.ds(group, step)].astype(f32)
        norm = lax.rsqrt(jnp.sum(tt * tt, axis=2, keepdims=True) + 1e-6)
        wcol[pl.ds(group, step)] = jnp.broadcast_to(norm, (step, MEMBERS, LANES))
        padded = jnp.concatenate([tt, jnp.zeros((step, MEMBERS, TIME - TPL), f32)], axis=2)
        for i in range(step):
            for k in range(MEMBERS):
                rows = jnp.broadcast_to(padded[i, k : k + 1], (SUB, TIME))
                tz[group + i, pl.ds(SUB * k, SUB), :] = pltpu.roll(rows, 0, 1, stride=1, stride_axis=0).astype(bf16)
        return carry

    lax.fori_loop(0, count // step, body, 0)


def number_rows(idx_ref, mask_ref, zh, mine, theirs, mcol):
    def body(g, carry):
        row0 = pl.multiple_of(8 * g, 8)
        for i in range(8):
            jc = 2 * g + i // 4
            k = i % 4
            j = jc // 3
            c = jc - 3 * j
            station = idx_ref[k, j]
            used = mask_ref[c, k, j]
            owner = station // PER
            half = owner // 8
            row = ((owner - 8 * half) * ROWS + c * PER + (station - PER * owner) + 1) * used
            here = half * zh + (1 - half) * (1 - zh)
            mine[pl.ds(row0 + i, 1), :] = jnp.full((1, LANES), (row * here).astype(f32), f32)
            theirs[pl.ds(row0 + i, 1), :] = jnp.full((1, LANES), (row * (1 - here)).astype(f32), f32)
            mcol[pl.ds(row0 + i, 1), :] = jnp.full((1, LANES), used.astype(f32), f32)
        return carry

    lax.fori_loop(0, GROUPS // 2, body, 0)


def band_matrix():
    u = lax.broadcasted_iota(i32, (768, LANES), 0)
    b = lax.broadcasted_iota(i32, (768, LANES), 1)
    d = u - b
    return jnp.where((d >= 0) & (d < TPL), 1.0, 0.0).astype(bf16)


def choose(rows, ids, base):
    number = lax.broadcasted_iota(i32, (TRACES, HALF), 1).astype(f32) + 1.0
    ids[pl.ds(base, TRACES), :] = jnp.where(jnp.broadcast_to(rows, (TRACES, HALF)) == number, 1.0, 0.0).astype(bf16)


def pick(ids, store, first, count):
    blocks = [store[:, first + i].reshape(HALF, LANES) for i in range(count)]
    return jnp.dot(ids, jnp.concatenate(blocks, axis=1), preferred_element_type=f32)


def spread(xs, wb, base):
    full = xs[pl.ds(base, TRACES), :]
    for a in range(4):
        moved = full if a == 0 else pltpu.roll(full, 2 * TIME - SUB * a, 1)
        for m in range(10):
            wb[pl.ds(40 * base + 4 * m + a, TRACES, stride=40), :] = moved[:, LANES * m : LANES * (m + 1)]


def window_scales(xs, band, sc, base):
    high, low = [], []
    for m in range(10):
        part = xs[pl.ds(base, TRACES), LANES * m : LANES * (m + 1)]
        square = part * part
        top = square.astype(bf16)
        high.append(top)
        low.append((square - top.astype(f32)).astype(bf16))
    lane = lax.broadcasted_iota(i32, (TRACES, LANES), 1) // SUB
    member = lax.rem(lax.broadcasted_iota(i32, (TRACES, LANES), 0), MEMBERS)
    for a in range(5):
        energy = jnp.dot(jnp.concatenate(high[a : a + 6], axis=1), band, preferred_element_type=f32)
        energy += jnp.dot(jnp.concatenate(low[a : a + 6], axis=1), band, preferred_element_type=f32)
        scale = lax.rsqrt(jnp.maximum(energy, 0.25 * TPL))
        turned = [scale] + [pltpu.roll(scale, SUB * d, 1) for d in range(1, 4)]
        for a2 in range(4):
            v = jnp.zeros((TRACES, LANES), f32)
            for k in range(MEMBERS):
                v = jnp.where((lane == k) & (member == k), turned[(k - a2) % 4], v)
            sc[pl.ds(24 * base + 4 * a + a2, TRACES, stride=24), :] = v


def correlate(tz, wb, sc, wcol, base, first, count, acc, unroll=9):
    def body(g, acc):
        for q in range(unroll):
            jc = first + g * unroll + q
            parts, gains = [], []
            for k in range(MEMBERS):
                row = pl.multiple_of((base + jc * MEMBERS + k) * 40, 8)
                parts.append(jnp.concatenate([wb[pl.ds(row + 4 * p, 24), :] for p in range(5)], axis=1))
                gains.append(jnp.broadcast_to(wcol[jc, k : k + 1, :], (24, LANES)))
            windows = jnp.concatenate(parts, axis=0).astype(bf16)
            c = lax.dot_general(windows, tz[jc], NT, preferred_element_type=f32)
            scale = sc[pl.ds(pl.multiple_of((base + jc * MEMBERS) * 24, 8), 96), :]
            acc = acc + c * (scale * jnp.concatenate(gains, axis=0))
        return acc

    return lax.fori_loop(0, count // unroll, body, acc)


def fold(acc):
    return (acc[0:24] + acc[24:48]) + (acc[48:72] + acc[72:96])


def finish(sums, mcol, o_ref):
    counts = jnp.sum(mcol[...].reshape(GROUPS, MEMBERS, LANES), axis=0)
    factor = jnp.sqrt(TPL / counts)
    lane = lax.broadcasted_iota(i32, (8, LANES), 1) // SUB
    quads = [sums[pl.ds(q, 5, stride=4), :] for q in range(4)]
    quads = [jnp.concatenate([rows, jnp.zeros((3, LANES), f32)], axis=0) for rows in quads]
    for k in range(MEMBERS):
        out = jnp.zeros((8, LANES), f32)
        for q in range(4):
            rows = quads[q] if q == k else pltpu.roll(quads[q], (SUB * (q - k)) % LANES, 1)
            out = jnp.where(lane == q, rows, out)
        for m in range(5):
            o_ref[k : k + 1, LANES * m : LANES * (m + 1)] = out[m : m + 1, :] * factor[k : k + 1, :]


def kernel(
    w_hbm, t_hbm, idx_hbm, mask_hbm, o_ref,
    w_ref, t_ref, idx_ref, mask_ref, t_far, n_out, n_in, gm, gh, ids, tz, tz_far, mine, theirs, wcol, wcol_far, mcol,
    xs, wb, sc, r_out, r_in, sums,
    in_sem, x_send, x_recv, s_send, s_recv, h_send, h_recv, t_send, t_recv, y_send, y_recv, n_send, n_recv, r_send, r_recv,
):
    blk, tm = lax.axis_index("blk"), lax.axis_index("tm")
    zh, x, core = blk // 8, lax.rem(blk // 2, 4), lax.rem(blk, 2)
    zl, y = tm // 4, lax.rem(tm, 4)

    def at(place, c):
        return lax.rem(place + 4, 4) * 2 + c

    loads = [
        pltpu.make_async_copy(src, dst, in_sem.at[i])
        for i, (src, dst) in enumerate(
            ((w_hbm, w_ref), (idx_hbm, idx_ref), (mask_hbm, mask_ref), (t_hbm, t_ref))
        )
    ]
    for load in loads:
        load.start()

    other = (1 - zh) * 8 + at(x, core)
    partner = (other, tm)
    mirror = (other, (7 - zl) * 4 + y)
    sibling = (zh * 8 + at(x, 1 - core), tm)
    across = [(zh * 8 + at(x + d, core), tm) for d in (1, -1, 2)]
    column = [(blk, zl * 4 + lax.rem(y + d + 4, 4)) for d in (1, -1, 2)]
    earlier, later = (blk, lax.rem(tm + 31, 32)), (blk, lax.rem(tm + 1, 32))
    has_earlier, has_later = tm > 0, tm < 31

    barrier = pltpu.get_barrier_semaphore()
    friends = (*across, *column, sibling, mirror, partner)
    for friend in friends:
        pl.semaphore_signal(barrier, inc=1, device_id=friend, device_id_type=MESH)

    @pl.when(has_earlier)
    def _():
        pl.semaphore_signal(barrier, inc=1, device_id=earlier, device_id_type=MESH)

    @pl.when(has_later)
    def _():
        pl.semaphore_signal(barrier, inc=1, device_id=later, device_id_type=MESH)

    loads[0].wait()
    own = w_ref[...].astype(f32)
    packed = jnp.concatenate([own[0], own[1], own[2], jnp.zeros((ROWS - 3 * PER, TIME), f32)], axis=0)
    slot = at(x, core)
    for m in range(5):
        gm[slot, m] = packed[:, LANES * m : LANES * (m + 1)].astype(bf16)
    pl.semaphore_wait(barrier, len(friends) + has_earlier.astype(i32) + has_later.astype(i32))

    def copy(src, dst, send, recv, to):
        return pltpu.make_async_remote_copy(
            src_ref=src, dst_ref=dst, send_sem=send, recv_sem=recv, device_id=to, device_id_type=MESH
        )

    store = (gm, gh)

    def x_copy(s, n):
        block = store[s].at[slot]
        return copy(block, block, x_send.at[s, n], x_recv.at[s, n], across[n])

    def x_wait(s, n):
        block = store[s].at[at(x + (-1, 1, 2)[n], core)]
        copy(block, block, x_send.at[s, n], x_recv.at[s, n], across[n]).wait_recv()

    def s_copy(s, n):
        block = store[s].at[at(x + (0, -1, 1, 2)[n], core)]
        return copy(block, block, s_send.at[s, n], s_recv.at[s, n], sibling)

    def s_wait(s):
        for n in range(4):
            block = store[s].at[at(x + (0, -1, 1, 2)[n], 1 - core)]
            copy(block, block, s_send.at[s, n], s_recv.at[s, n], sibling).wait_recv()

    facing = at(x + 2, core)
    h_copies = [
        copy(gm.at[place], gh.at[place], h_send.at[n], h_recv.at[n], earlier) for n, place in enumerate((slot, facing))
    ]

    def h_start(n):
        @pl.when(has_earlier)
        def _():
            h_copies[n].start()

    def h_wait(n):
        @pl.when(has_later)
        def _():
            h_copies[n].wait_recv()

        @pl.when(jnp.logical_not(has_later))
        def _():
            for m in range(5):
                gh[(slot, facing)[n], m] = jnp.zeros((ROWS, LANES), bf16)


    def quarter(ref, part):
        return ref.at[pl.ds(QUARTER * lax.rem(part + 4, 4), QUARTER)]

    t_copy = copy(quarter(t_hbm, y), quarter(t_far, y), t_send, t_recv, mirror)

    def y_copy(n):
        block = quarter(t_far, y)
        return copy(block, block, y_send.at[n], y_recv.at[n], column[n])

    def y_wait(n):
        block = quarter(t_far, y + (-1, 1, 2)[n])
        copy(block, block, y_send.at[n], y_recv.at[n], column[n]).wait_recv()

    n_copy = copy(n_out, n_in, n_send, n_recv, mirror)
    r_copy = copy(r_out, r_in, r_send, r_recv, partner)

    t_copy.start()
    h_start(0)
    for n in (2, 0, 1):
        x_copy(0, n).start()
    s_copy(0, 0).start()
    loads[1].wait()
    loads[2].wait()
    number_rows(idx_ref, mask_ref, zh, mine, theirs, mcol)
    flat = jnp.transpose(theirs[...])[0:8, :]
    sixteens = jnp.floor(flat * (1.0 / 16.0))
    n_out[...] = jnp.concatenate([sixteens, flat - 16.0 * sixteens], axis=0).astype(bf16)
    n_copy.start()
    choose(mine[0:TRACES, 0:1], ids, 0)
    loads[3].wait()
    build_toeplitz(t_ref, tz, wcol, 0, GROUPS)
    h_wait(0)
    for n in range(2):
        x_copy(1, n).start()
    s_copy(1, 0).start()
    x_wait(0, 2)
    h_start(1)
    s_copy(0, 3).start()
    t_copy.wait_recv()
    for n in range(3):
        y_copy(n).start()
    for n in range(2):
        x_wait(0, n)
        s_copy(0, 1 + n).start()
    build_toeplitz(t_far, tz_far, wcol_far, QUARTER * y, QUARTER)
    n_copy.wait_recv()
    got = n_in[...].astype(f32)
    choose(jnp.transpose(got[0:8] * 16.0 + got[8:16])[0:TRACES, 0:1], ids, TRACES)
    h_wait(1)
    s_copy(1, 3).start()
    for n in range(2):
        x_wait(1, n)
        s_copy(1, 1 + n).start()
    s_wait(0)
    xs[:, :TIME] = pick(ids[...], gm, 0, 5)
    band = band_matrix()
    for n in range(3):
        y_wait(n)
        build_toeplitz(t_far, tz_far, wcol_far, QUARTER * lax.rem(y + (3, 1, 2)[n], 4), QUARTER)
    s_wait(1)
    xs[pl.ds(TRACES, TRACES), TIME:] = pick(ids[pl.ds(TRACES, TRACES), :], gh, 0, 5)
    spread(xs, wb, TRACES)
    window_scales(xs, band, sc, TRACES)
    acc = jnp.zeros((96, LANES), f32)
    acc = correlate(tz_far, wb, sc, wcol_far, TRACES, 0, GROUPS, acc, 36)
    r_out[...] = fold(acc)
    r_copy.start()
    xs[pl.ds(0, TRACES), TIME:] = pick(ids[pl.ds(0, TRACES), :], gh, 0, 5)
    spread(xs, wb, 0)
    window_scales(xs, band, sc, 0)
    total = fold(correlate(tz, wb, sc, wcol, 0, 0, GROUPS, jnp.zeros((96, LANES), f32), 12))
    r_copy.wait_recv()
    sums[...] = total + r_in[...]
    finish(sums, mcol, o_ref)

    for n in range(3):
        y_copy(n).wait_send()
        x_copy(0, n).wait_send()
    for n in range(2):
        x_copy(1, n).wait_send()
    for n in range(4):
        for s in range(2):
            s_copy(s, n).wait_send()
    for sent in (t_copy, n_copy, r_copy):
        sent.wait_send()

    @pl.when(has_earlier)
    def _():
        for h in h_copies:
            h.wait_send()


def per_device(waveform, templates, station_index, channel_mask):
    w = jnp.transpose(waveform, (1, 0, 2))
    t = jnp.transpose(templates, (1, 2, 0, 3)).reshape(GROUPS, MEMBERS, TPL)
    mask = jnp.transpose(channel_mask, (2, 0, 1))
    anywhere = pl.BlockSpec(memory_space=pl.ANY)
    dma = pltpu.SemaphoreType.DMA
    return pl.pallas_call(
        kernel,
        out_shape=jax.ShapeDtypeStruct((MEMBERS, TIME), f32),
        in_specs=[anywhere] * 4,
        out_specs=pl.BlockSpec(memory_space=pltpu.VMEM),
        scratch_shapes=[
            pltpu.VMEM(w.shape, bf16),
            pltpu.VMEM(t.shape, bf16),
            pltpu.SMEM(station_index.shape, i32),
            pltpu.SMEM(mask.shape, i32),
            pltpu.VMEM(t.shape, bf16),
            pltpu.VMEM((16, 256), bf16),
            pltpu.VMEM((16, 256), bf16),
            pltpu.VMEM((SLOTS, 5, ROWS, LANES), bf16),
            pltpu.VMEM((SLOTS, 5, ROWS, LANES), bf16),
            pltpu.VMEM((2 * TRACES, HALF), bf16),
            pltpu.VMEM((GROUPS, LANES, TIME), bf16),
            pltpu.VMEM((GROUPS, LANES, TIME), bf16),
            pltpu.VMEM((256, LANES), f32),
            pltpu.VMEM((256, LANES), f32),
            pltpu.VMEM((GROUPS, MEMBERS, LANES), f32),
            pltpu.VMEM((GROUPS, MEMBERS, LANES), f32),
            pltpu.VMEM((TRACES, LANES), f32),
            pltpu.VMEM((2 * TRACES, 2 * TIME), f32),
            pltpu.VMEM((2 * TRACES * 40, LANES), f32),
            pltpu.VMEM((2 * TRACES * 24, LANES), f32),
            pltpu.VMEM((24, LANES), f32),
            pltpu.VMEM((24, LANES), f32),
            pltpu.VMEM((24, LANES), f32),
            dma((4,)),
            dma((2, 3)),
            dma((2, 3)),
            dma((2, 4)),
            dma((2, 4)),
            dma((2,)),
            dma((2,)),
            dma,
            dma,
            dma((3,)),
            dma((3,)),
            dma,
            dma,
            dma,
            dma,
        ],
        compiler_params=pltpu.CompilerParams(
            collective_id=0, has_side_effects=True, vmem_limit_bytes=56 * 2**20
        ),
    )(w, t, station_index, mask)


def solution(mesh):
    return jax.shard_map(
        per_device,
        mesh=mesh,
        in_specs=(
            P("blk", None, "tm"),
            P("blk", None, None, None),
            P("blk", None),
            P("blk", None, None),
        ),
        out_specs=P("blk", "tm"),
        check_vma=False,
    )
```

```python
import jax
import jax.numpy as jnp
from jax import lax
from jax.experimental import pallas as pl
from jax.experimental.pallas import tpu as pltpu
from jax.sharding import PartitionSpec as P

bf16, f32, i32 = jnp.bfloat16, jnp.float32, jnp.int32
MESH = pl.DeviceIdType.MESH
NT = (((1,), (1,)), ((), ()))

TPL = 600
TIME = 640
PER = 25
ROWS = 80
SUB = 32
LANES = 128
GROUPS = 36
MEMBERS = 4
TRACES = GROUPS * MEMBERS
HALF = 8 * ROWS
SLOTS = 8
QUARTER = GROUPS // 4
PIECE = QUARTER // 3


def build_toeplitz(t_ref, tz, wcol, first, count, step=3):
    def body(g, carry):
        group = first + step * g
        tt = t_ref[pl.ds(group, step)].astype(f32)
        norm = lax.rsqrt(jnp.sum(tt * tt, axis=2, keepdims=True) + 1e-6)
        wcol[pl.ds(group, step)] = jnp.broadcast_to(norm, (step, MEMBERS, LANES))
        padded = jnp.concatenate([tt, jnp.zeros((step, MEMBERS, TIME - TPL), f32)], axis=2)
        for i in range(step):
            for k in range(MEMBERS):
                rows = jnp.broadcast_to(padded[i, k : k + 1], (SUB, TIME))
                tz[group + i, pl.ds(SUB * k, SUB), :] = pltpu.roll(rows, 0, 1, stride=1, stride_axis=0).astype(bf16)
        return carry

    lax.fori_loop(0, count // step, body, 0)


def number_rows(idx_ref, mask_ref, zh, mine, theirs, mcol):
    def body(g, carry):
        row0 = pl.multiple_of(8 * g, 8)
        for i in range(8):
            jc = 2 * g + i // 4
            k = i % 4
            j = jc // 3
            c = jc - 3 * j
            station = idx_ref[k, j]
            used = mask_ref[c, k, j]
            owner = station // PER
            half = owner // 8
            row = ((owner - 8 * half) * ROWS + c * PER + (station - PER * owner) + 1) * used
            here = half * zh + (1 - half) * (1 - zh)
            mine[pl.ds(row0 + i, 1), :] = jnp.full((1, LANES), (row * here).astype(f32), f32)
            theirs[pl.ds(row0 + i, 1), :] = jnp.full((1, LANES), (row * (1 - here)).astype(f32), f32)
            mcol[pl.ds(row0 + i, 1), :] = jnp.full((1, LANES), used.astype(f32), f32)
        return carry

    lax.fori_loop(0, GROUPS // 2, body, 0)


def band_matrix():
    u = lax.broadcasted_iota(i32, (768, LANES), 0)
    b = lax.broadcasted_iota(i32, (768, LANES), 1)
    d = u - b
    return jnp.where((d >= 0) & (d < TPL), 1.0, 0.0).astype(bf16)


def choose(rows, ids, base):
    number = lax.broadcasted_iota(i32, (TRACES, HALF), 1).astype(f32) + 1.0
    ids[pl.ds(base, TRACES), :] = jnp.where(jnp.broadcast_to(rows, (TRACES, HALF)) == number, 1.0, 0.0).astype(bf16)


def pick(ids, store, first, count):
    blocks = [store[:, first + i].reshape(HALF, LANES) for i in range(count)]
    return jnp.dot(ids, jnp.concatenate(blocks, axis=1), preferred_element_type=f32)


def spread(xs, wb, base):
    full = xs[pl.ds(base, TRACES), :]
    for a in range(4):
        moved = full if a == 0 else pltpu.roll(full, 2 * TIME - SUB * a, 1)
        for m in range(10):
            wb[pl.ds(40 * base + 4 * m + a, TRACES, stride=40), :] = moved[:, LANES * m : LANES * (m + 1)]


def window_scales(xs, band, sc, base):
    high, low = [], []
    for m in range(10):
        part = xs[pl.ds(base, TRACES), LANES * m : LANES * (m + 1)]
        square = part * part
        top = square.astype(bf16)
        high.append(top)
        low.append((square - top.astype(f32)).astype(bf16))
    lane = lax.broadcasted_iota(i32, (TRACES, LANES), 1) // SUB
    member = lax.rem(lax.broadcasted_iota(i32, (TRACES, LANES), 0), MEMBERS)
    for a in range(5):
        energy = jnp.dot(jnp.concatenate(high[a : a + 6], axis=1), band, preferred_element_type=f32)
        energy += jnp.dot(jnp.concatenate(low[a : a + 6], axis=1), band, preferred_element_type=f32)
        scale = lax.rsqrt(jnp.maximum(energy, 0.25 * TPL))
        turned = [scale] + [pltpu.roll(scale, SUB * d, 1) for d in range(1, 4)]
        for a2 in range(4):
            v = jnp.zeros((TRACES, LANES), f32)
            for k in range(MEMBERS):
                v = jnp.where((lane == k) & (member == k), turned[(k - a2) % 4], v)
            sc[pl.ds(24 * base + 4 * a + a2, TRACES, stride=24), :] = v


def correlate(tz, wb, sc, wcol, base, first, count, acc, unroll=9):
    def body(g, acc):
        for q in range(unroll):
            jc = first + g * unroll + q
            parts, gains = [], []
            for k in range(MEMBERS):
                row = pl.multiple_of((base + jc * MEMBERS + k) * 40, 8)
                parts.append(jnp.concatenate([wb[pl.ds(row + 4 * p, 24), :] for p in range(5)], axis=1))
                gains.append(jnp.broadcast_to(wcol[jc, k : k + 1, :], (24, LANES)))
            windows = jnp.concatenate(parts, axis=0).astype(bf16)
            c = lax.dot_general(windows, tz[jc], NT, preferred_element_type=f32)
            scale = sc[pl.ds(pl.multiple_of((base + jc * MEMBERS) * 24, 8), 96), :]
            acc = acc + c * (scale * jnp.concatenate(gains, axis=0))
        return acc

    return lax.fori_loop(0, count // unroll, body, acc)


def fold(acc):
    return (acc[0:24] + acc[24:48]) + (acc[48:72] + acc[72:96])


def finish(sums, mcol, o_ref):
    counts = jnp.sum(mcol[...].reshape(GROUPS, MEMBERS, LANES), axis=0)
    factor = jnp.sqrt(TPL / counts)
    lane = lax.broadcasted_iota(i32, (8, LANES), 1) // SUB
    quads = [sums[pl.ds(q, 5, stride=4), :] for q in range(4)]
    quads = [jnp.concatenate([rows, jnp.zeros((3, LANES), f32)], axis=0) for rows in quads]
    for k in range(MEMBERS):
        out = jnp.zeros((8, LANES), f32)
        for q in range(4):
            rows = quads[q] if q == k else pltpu.roll(quads[q], (SUB * (q - k)) % LANES, 1)
            out = jnp.where(lane == q, rows, out)
        for m in range(5):
            o_ref[k : k + 1, LANES * m : LANES * (m + 1)] = out[m : m + 1, :] * factor[k : k + 1, :]


def kernel(
    w_hbm, t_hbm, idx_hbm, mask_hbm, o_ref,
    w_ref, t_ref, idx_ref, mask_ref, t_far, n_out, n_in, gm, gh, ids, tz, tz_far, mine, theirs, wcol, wcol_far, mcol,
    xs, wb, sc, r_out, r_in, sums,
    in_sem, x_send, x_recv, s_send, s_recv, h_send, h_recv, t_send, t_recv, y_send, y_recv, n_send, n_recv, r_send, r_recv, meet,
):
    blk, tm = lax.axis_index("blk"), lax.axis_index("tm")
    zh, x, core = blk // 8, lax.rem(blk // 2, 4), lax.rem(blk, 2)
    zl, y = tm // 4, lax.rem(tm, 4)

    def at(place, c):
        return lax.rem(place + 4, 4) * 2 + c

    loads = [
        pltpu.make_async_copy(src, dst, in_sem.at[i])
        for i, (src, dst) in enumerate(
            ((w_hbm, w_ref), (idx_hbm, idx_ref), (mask_hbm, mask_ref), (t_hbm, t_ref))
        )
    ]
    for load in loads:
        load.start()

    other = (1 - zh) * 8 + at(x, core)
    partner = (other, tm)
    mirror = (other, (7 - zl) * 4 + y)
    sibling = (zh * 8 + at(x, 1 - core), tm)
    across = [(zh * 8 + at(x + d, core), tm) for d in (1, -1, 2)]
    column = [(blk, zl * 4 + lax.rem(y + d + 4, 4)) for d in (1, -1, 2)]
    earlier, later = (blk, lax.rem(tm + 31, 32)), (blk, lax.rem(tm + 1, 32))
    has_earlier, has_later = tm > 0, tm < 31

    barrier = pltpu.get_barrier_semaphore()
    friends = (*across, *column, sibling, mirror)
    for friend in friends:
        pl.semaphore_signal(barrier, inc=1, device_id=friend, device_id_type=MESH)

    first_half = zh == 0

    @pl.when(first_half)
    def _():
        pl.semaphore_signal(barrier, inc=1, device_id=partner, device_id_type=MESH)

    @pl.when(has_earlier)
    def _():
        pl.semaphore_signal(barrier, inc=1, device_id=earlier, device_id_type=MESH)

    @pl.when(has_later)
    def _():
        pl.semaphore_signal(barrier, inc=1, device_id=later, device_id_type=MESH)

    loads[0].wait()
    own = w_ref[...].astype(f32)
    packed = jnp.concatenate([own[0], own[1], own[2], jnp.zeros((ROWS - 3 * PER, TIME), f32)], axis=0)
    slot = at(x, core)
    for m in range(5):
        gm[slot, m] = packed[:, LANES * m : LANES * (m + 1)].astype(bf16)
    pl.semaphore_wait(barrier, len(friends) + zh + has_earlier.astype(i32) + has_later.astype(i32))

    @pl.when(jnp.logical_not(first_half))
    def _():
        pl.semaphore_signal(meet, inc=1, device_id=partner, device_id_type=MESH)

    def copy(src, dst, send, recv, to):
        return pltpu.make_async_remote_copy(
            src_ref=src, dst_ref=dst, send_sem=send, recv_sem=recv, device_id=to, device_id_type=MESH
        )

    store = (gm, gh)

    def x_copy(s, n):
        block = store[s].at[slot]
        return copy(block, block, x_send.at[s, n], x_recv.at[s, n], across[n])

    def x_wait(s, n):
        block = store[s].at[at(x + (-1, 1, 2)[n], core)]
        copy(block, block, x_send.at[s, n], x_recv.at[s, n], across[n]).wait_recv()

    def s_copy(s, n):
        block = store[s].at[at(x + (0, -1, 1, 2)[n], core)]
        return copy(block, block, s_send.at[s, n], s_recv.at[s, n], sibling)

    def s_wait(s):
        for n in range(4):
            block = store[s].at[at(x + (0, -1, 1, 2)[n], 1 - core)]
            copy(block, block, s_send.at[s, n], s_recv.at[s, n], sibling).wait_recv()

    facing = at(x + 2, core)
    h_copies = [
        copy(gm.at[place], gh.at[place], h_send.at[n], h_recv.at[n], earlier) for n, place in enumerate((slot, facing))
    ]

    def h_start(n):
        @pl.when(has_earlier)
        def _():
            h_copies[n].start()

    def h_wait(n):
        @pl.when(has_later)
        def _():
            h_copies[n].wait_recv()

        @pl.when(jnp.logical_not(has_later))
        def _():
            for m in range(5):
                gh[(slot, facing)[n], m] = jnp.zeros((ROWS, LANES), bf16)


    def piece(ref, part, p):
        return ref.at[pl.ds(QUARTER * lax.rem(part + 4, 4) + PIECE * p, PIECE)]

    def t_copy(p):
        return copy(piece(t_hbm, y, p), piece(t_far, y, p), t_send.at[p], t_recv.at[p], mirror)

    def y_copy(p, n):
        block = piece(t_far, y, p)
        return copy(block, block, y_send.at[p, n], y_recv.at[p, n], column[n])

    def y_pass(p):
        t_copy(p).wait_recv()
        for n in (2, 0, 1):
            y_copy(p, n).start()

    def y_build(p):
        for n in range(3):
            part = y + (-1, 1, 2)[n]
            block = piece(t_far, part, p)
            copy(block, block, y_send.at[p, n], y_recv.at[p, n], column[n]).wait_recv()
            build_toeplitz(t_far, tz_far, wcol_far, QUARTER * lax.rem(part + 4, 4) + PIECE * p, PIECE)

    n_copy = copy(n_out, n_in, n_send, n_recv, mirror)
    r_copy = copy(r_out, r_in, r_send, r_recv, partner)

    for p in range(3):
        t_copy(p).start()
    h_start(0)
    for n in (2, 0, 1):
        x_copy(0, n).start()
    s_copy(0, 0).start()
    loads[1].wait()
    loads[2].wait()
    number_rows(idx_ref, mask_ref, zh, mine, theirs, mcol)
    flat = jnp.transpose(theirs[...])[0:8, :]
    sixteens = jnp.floor(flat * (1.0 / 16.0))
    n_out[...] = jnp.concatenate([sixteens, flat - 16.0 * sixteens], axis=0).astype(bf16)
    n_copy.start()
    choose(mine[0:TRACES, 0:1], ids, 0)
    loads[3].wait()
    build_toeplitz(t_ref, tz, wcol, 0, GROUPS)
    h_wait(0)
    for n in range(2):
        x_copy(1, n).start()
    s_copy(1, 0).start()
    y_pass(0)
    x_wait(0, 2)
    h_start(1)
    s_copy(0, 3).start()
    y_pass(1)
    for n in range(2):
        x_wait(0, n)
        s_copy(0, 1 + n).start()
    y_pass(2)
    build_toeplitz(t_far, tz_far, wcol_far, QUARTER * y, QUARTER)
    n_copy.wait_recv()
    got = n_in[...].astype(f32)
    choose(jnp.transpose(got[0:8] * 16.0 + got[8:16])[0:TRACES, 0:1], ids, TRACES)
    y_build(0)
    h_wait(1)
    s_copy(1, 3).start()
    for n in range(2):
        x_wait(1, n)
        s_copy(1, 1 + n).start()
    y_build(1)
    s_wait(0)
    xs[:, :TIME] = pick(ids[...], gm, 0, 5)
    band = band_matrix()
    y_build(2)
    s_wait(1)
    xs[pl.ds(TRACES, TRACES), TIME:] = pick(ids[pl.ds(TRACES, TRACES), :], gh, 0, 5)
    spread(xs, wb, TRACES)
    window_scales(xs, band, sc, TRACES)
    acc = jnp.zeros((96, LANES), f32)
    acc = correlate(tz_far, wb, sc, wcol_far, TRACES, 0, GROUPS, acc, 36)
    r_out[...] = fold(acc)

    @pl.when(first_half)
    def _():
        pl.semaphore_wait(meet, 1)

    r_copy.start()
    xs[pl.ds(0, TRACES), TIME:] = pick(ids[pl.ds(0, TRACES), :], gh, 0, 5)
    spread(xs, wb, 0)
    window_scales(xs, band, sc, 0)
    total = fold(correlate(tz, wb, sc, wcol, 0, 0, GROUPS, jnp.zeros((96, LANES), f32), 12))
    r_copy.wait_recv()
    sums[...] = total + r_in[...]
    finish(sums, mcol, o_ref)

    for p in range(3):
        t_copy(p).wait_send()
        for n in range(3):
            y_copy(p, n).wait_send()
    for n in range(3):
        x_copy(0, n).wait_send()
    for n in range(2):
        x_copy(1, n).wait_send()
    for n in range(4):
        for s in range(2):
            s_copy(s, n).wait_send()
    for sent in (n_copy, r_copy):
        sent.wait_send()

    @pl.when(has_earlier)
    def _():
        for h in h_copies:
            h.wait_send()


def per_device(waveform, templates, station_index, channel_mask):
    w = jnp.transpose(waveform, (1, 0, 2))
    t = jnp.transpose(templates, (1, 2, 0, 3)).reshape(GROUPS, MEMBERS, TPL)
    mask = jnp.transpose(channel_mask, (2, 0, 1))
    anywhere = pl.BlockSpec(memory_space=pl.ANY)
    dma = pltpu.SemaphoreType.DMA
    return pl.pallas_call(
        kernel,
        out_shape=jax.ShapeDtypeStruct((MEMBERS, TIME), f32),
        in_specs=[anywhere] * 4,
        out_specs=pl.BlockSpec(memory_space=pltpu.VMEM),
        scratch_shapes=[
            pltpu.VMEM(w.shape, bf16),
            pltpu.VMEM(t.shape, bf16),
            pltpu.SMEM(station_index.shape, i32),
            pltpu.SMEM(mask.shape, i32),
            pltpu.VMEM(t.shape, bf16),
            pltpu.VMEM((16, 256), bf16),
            pltpu.VMEM((16, 256), bf16),
            pltpu.VMEM((SLOTS, 5, ROWS, LANES), bf16),
            pltpu.VMEM((SLOTS, 5, ROWS, LANES), bf16),
            pltpu.VMEM((2 * TRACES, HALF), bf16),
            pltpu.VMEM((GROUPS, LANES, TIME), bf16),
            pltpu.VMEM((GROUPS, LANES, TIME), bf16),
            pltpu.VMEM((256, LANES), f32),
            pltpu.VMEM((256, LANES), f32),
            pltpu.VMEM((GROUPS, MEMBERS, LANES), f32),
            pltpu.VMEM((GROUPS, MEMBERS, LANES), f32),
            pltpu.VMEM((TRACES, LANES), f32),
            pltpu.VMEM((2 * TRACES, 2 * TIME), f32),
            pltpu.VMEM((2 * TRACES * 40, LANES), f32),
            pltpu.VMEM((2 * TRACES * 24, LANES), f32),
            pltpu.VMEM((24, LANES), f32),
            pltpu.VMEM((24, LANES), f32),
            pltpu.VMEM((24, LANES), f32),
            dma((4,)),
            dma((2, 3)),
            dma((2, 3)),
            dma((2, 4)),
            dma((2, 4)),
            dma((2,)),
            dma((2,)),
            dma((3,)),
            dma((3,)),
            dma((3, 3)),
            dma((3, 3)),
            dma,
            dma,
            dma,
            dma,
            pltpu.SemaphoreType.REGULAR,
        ],
        compiler_params=pltpu.CompilerParams(
            collective_id=0, has_side_effects=True, vmem_limit_bytes=56 * 2**20
        ),
    )(w, t, station_index, mask)


def solution(mesh):
    return jax.shard_map(
        per_device,
        mesh=mesh,
        in_specs=(
            P("blk", None, "tm"),
            P("blk", None, None, None),
            P("blk", None),
            P("blk", None, None),
        ),
        out_specs=P("blk", "tm"),
        check_vma=False,
    )
```

```python
import jax
import jax.numpy as jnp
from jax import lax
from jax.experimental import pallas as pl
from jax.experimental.pallas import tpu as pltpu
from jax.sharding import PartitionSpec as P

bf16, f32, i32 = jnp.bfloat16, jnp.float32, jnp.int32
MESH = pl.DeviceIdType.MESH
NT = (((1,), (1,)), ((), ()))

TPL = 600
TIME = 640
PER = 25
ROWS = 80
SUB = 32
LANES = 128
GROUPS = 36
MEMBERS = 4
TRACES = GROUPS * MEMBERS
HALF = 8 * ROWS
SLOTS = 8
QUARTER = GROUPS // 4
PIECE = QUARTER // 3


def build_toeplitz(t_ref, tz, wcol, first, count, step=3):
    def body(g, carry):
        group = first + step * g
        tt = t_ref[pl.ds(group, step)].astype(f32)
        norm = lax.rsqrt(jnp.sum(tt * tt, axis=2, keepdims=True) + 1e-6)
        wcol[pl.ds(group, step)] = jnp.broadcast_to(norm, (step, MEMBERS, LANES))
        padded = jnp.concatenate([tt, jnp.zeros((step, MEMBERS, TIME - TPL), f32)], axis=2)
        for i in range(step):
            for k in range(MEMBERS):
                rows = jnp.broadcast_to(padded[i, k : k + 1], (SUB, TIME))
                tz[group + i, pl.ds(SUB * k, SUB), :] = pltpu.roll(rows, 0, 1, stride=1, stride_axis=0).astype(bf16)
        return carry

    lax.fori_loop(0, count // step, body, 0)


def number_rows(idx_ref, mask_ref, zh, mine, theirs, mcol):
    def body(g, carry):
        row0 = pl.multiple_of(8 * g, 8)
        for i in range(8):
            jc = 2 * g + i // 4
            k = i % 4
            j = jc // 3
            c = jc - 3 * j
            station = idx_ref[k, j]
            used = mask_ref[c, k, j]
            owner = station // PER
            half = owner // 8
            row = ((owner - 8 * half) * ROWS + c * PER + (station - PER * owner) + 1) * used
            here = half * zh + (1 - half) * (1 - zh)
            mine[pl.ds(row0 + i, 1), :] = jnp.full((1, LANES), (row * here).astype(f32), f32)
            theirs[pl.ds(row0 + i, 1), :] = jnp.full((1, LANES), (row * (1 - here)).astype(f32), f32)
            mcol[pl.ds(row0 + i, 1), :] = jnp.full((1, LANES), used.astype(f32), f32)
        return carry

    lax.fori_loop(0, GROUPS // 2, body, 0)


def band_matrix():
    u = lax.broadcasted_iota(i32, (768, LANES), 0)
    b = lax.broadcasted_iota(i32, (768, LANES), 1)
    d = u - b
    return jnp.where((d >= 0) & (d < TPL), 1.0, 0.0).astype(bf16)


def choose(rows, ids, base):
    number = lax.broadcasted_iota(i32, (TRACES, HALF), 1).astype(f32) + 1.0
    ids[pl.ds(base, TRACES), :] = jnp.where(jnp.broadcast_to(rows, (TRACES, HALF)) == number, 1.0, 0.0).astype(bf16)


def pick(ids, store, first, count):
    blocks = [store[:, first + i].reshape(HALF, LANES) for i in range(count)]
    return jnp.dot(ids, jnp.concatenate(blocks, axis=1), preferred_element_type=f32)


def spread(xs, wb, base):
    full = xs[pl.ds(base, TRACES), :]
    for a in range(4):
        moved = full if a == 0 else pltpu.roll(full, 2 * TIME - SUB * a, 1)
        for m in range(10):
            wb[pl.ds(40 * base + 4 * m + a, TRACES, stride=40), :] = moved[:, LANES * m : LANES * (m + 1)]


def window_scales(xs, band, sc, base):
    high, low = [], []
    for m in range(10):
        part = xs[pl.ds(base, TRACES), LANES * m : LANES * (m + 1)]
        square = part * part
        top = square.astype(bf16)
        high.append(top)
        low.append((square - top.astype(f32)).astype(bf16))
    lane = lax.broadcasted_iota(i32, (TRACES, LANES), 1) // SUB
    member = lax.rem(lax.broadcasted_iota(i32, (TRACES, LANES), 0), MEMBERS)
    for a in range(5):
        energy = jnp.dot(jnp.concatenate(high[a : a + 6], axis=1), band, preferred_element_type=f32)
        energy += jnp.dot(jnp.concatenate(low[a : a + 6], axis=1), band, preferred_element_type=f32)
        scale = lax.rsqrt(jnp.maximum(energy, 0.25 * TPL))
        turned = [scale] + [pltpu.roll(scale, SUB * d, 1) for d in range(1, 4)]
        for a2 in range(4):
            v = jnp.zeros((TRACES, LANES), f32)
            for k in range(MEMBERS):
                v = jnp.where((lane == k) & (member == k), turned[(k - a2) % 4], v)
            sc[pl.ds(24 * base + 4 * a + a2, TRACES, stride=24), :] = v


def correlate(tz, wb, sc, wcol, base, first, count, acc, unroll=9):
    def body(g, acc):
        for q in range(unroll):
            jc = first + g * unroll + q
            parts, gains = [], []
            for k in range(MEMBERS):
                row = pl.multiple_of((base + jc * MEMBERS + k) * 40, 8)
                parts.append(jnp.concatenate([wb[pl.ds(row + 4 * p, 24), :] for p in range(5)], axis=1))
                gains.append(jnp.broadcast_to(wcol[jc, k : k + 1, :], (24, LANES)))
            windows = jnp.concatenate(parts, axis=0).astype(bf16)
            c = lax.dot_general(windows, tz[jc], NT, preferred_element_type=f32)
            scale = sc[pl.ds(pl.multiple_of((base + jc * MEMBERS) * 24, 8), 96), :]
            acc = acc + c * (scale * jnp.concatenate(gains, axis=0))
        return acc

    return lax.fori_loop(0, count // unroll, body, acc)


def fold(acc):
    return (acc[0:24] + acc[24:48]) + (acc[48:72] + acc[72:96])


def finish(sums, mcol, o_ref):
    counts = jnp.sum(mcol[...].reshape(GROUPS, MEMBERS, LANES), axis=0)
    factor = jnp.sqrt(TPL / counts)
    lane = lax.broadcasted_iota(i32, (8, LANES), 1) // SUB
    quads = [sums[pl.ds(q, 5, stride=4), :] for q in range(4)]
    quads = [jnp.concatenate([rows, jnp.zeros((3, LANES), f32)], axis=0) for rows in quads]
    for k in range(MEMBERS):
        out = jnp.zeros((8, LANES), f32)
        for q in range(4):
            rows = quads[q] if q == k else pltpu.roll(quads[q], (SUB * (q - k)) % LANES, 1)
            out = jnp.where(lane == q, rows, out)
        for m in range(5):
            o_ref[k : k + 1, LANES * m : LANES * (m + 1)] = out[m : m + 1, :] * factor[k : k + 1, :]


def kernel(
    w_hbm, t_hbm, idx_hbm, mask_hbm, o_ref,
    w_ref, t_ref, idx_ref, mask_ref, t_far, n_out, n_in, gm, gh, ids, tz, tz_far, mine, theirs, wcol, wcol_far, mcol,
    xs, wb, sc, r_out, r_in, sums,
    in_sem, x_send, x_recv, s_send, s_recv, h_send, h_recv, t_send, t_recv, y_send, y_recv, n_send, n_recv, r_send, r_recv, meet,
):
    blk, tm = lax.axis_index("blk"), lax.axis_index("tm")
    zh, x, core = blk // 8, lax.rem(blk // 2, 4), lax.rem(blk, 2)
    zl, y = tm // 4, lax.rem(tm, 4)

    def at(place, c):
        return lax.rem(place + 4, 4) * 2 + c

    loads = [
        pltpu.make_async_copy(src, dst, in_sem.at[i])
        for i, (src, dst) in enumerate(
            ((w_hbm, w_ref), (idx_hbm, idx_ref), (mask_hbm, mask_ref), (t_hbm, t_ref))
        )
    ]
    loads[0].start()

    other = (1 - zh) * 8 + at(x, core)
    partner = (other, tm)
    mirror = (other, (7 - zl) * 4 + y)
    sibling = (zh * 8 + at(x, 1 - core), tm)
    across = [(zh * 8 + at(x + d, core), tm) for d in (1, -1, 2)]
    column = [(blk, zl * 4 + lax.rem(y + d + 4, 4)) for d in (1, -1, 2)]
    earlier, later = (blk, lax.rem(tm + 31, 32)), (blk, lax.rem(tm + 1, 32))
    has_earlier, has_later = tm > 0, tm < 31

    barrier = pltpu.get_barrier_semaphore()
    friends = (mirror, *across, *column, sibling)
    for friend in friends:
        pl.semaphore_signal(barrier, inc=1, device_id=friend, device_id_type=MESH)

    first_half = zh == 0

    @pl.when(first_half)
    def _():
        pl.semaphore_signal(barrier, inc=1, device_id=partner, device_id_type=MESH)

    @pl.when(has_earlier)
    def _():
        pl.semaphore_signal(barrier, inc=1, device_id=earlier, device_id_type=MESH)

    @pl.when(has_later)
    def _():
        pl.semaphore_signal(barrier, inc=1, device_id=later, device_id_type=MESH)

    for load in loads[1:]:
        load.start()
    loads[0].wait()
    own = w_ref[...].astype(f32)
    packed = jnp.concatenate([own[0], own[1], own[2], jnp.zeros((ROWS - 3 * PER, TIME), f32)], axis=0)
    slot = at(x, core)
    for m in range(5):
        gm[slot, m] = packed[:, LANES * m : LANES * (m + 1)].astype(bf16)
    pl.semaphore_wait(barrier, len(friends) + zh + has_earlier.astype(i32) + has_later.astype(i32))

    @pl.when(jnp.logical_not(first_half))
    def _():
        pl.semaphore_signal(meet, inc=1, device_id=partner, device_id_type=MESH)

    def copy(src, dst, send, recv, to):
        return pltpu.make_async_remote_copy(
            src_ref=src, dst_ref=dst, send_sem=send, recv_sem=recv, device_id=to, device_id_type=MESH
        )

    store = (gm, gh)

    def x_copy(s, n):
        block = store[s].at[slot]
        return copy(block, block, x_send.at[s, n], x_recv.at[s, n], across[n])

    def x_wait(s, n):
        block = store[s].at[at(x + (-1, 1, 2)[n], core)]
        copy(block, block, x_send.at[s, n], x_recv.at[s, n], across[n]).wait_recv()

    def s_copy(s, n):
        block = store[s].at[at(x + (0, -1, 1, 2)[n], core)]
        return copy(block, block, s_send.at[s, n], s_recv.at[s, n], sibling)

    def s_wait(s):
        for n in range(4):
            block = store[s].at[at(x + (0, -1, 1, 2)[n], 1 - core)]
            copy(block, block, s_send.at[s, n], s_recv.at[s, n], sibling).wait_recv()

    facing = at(x + 2, core)
    h_copies = [
        copy(gm.at[place], gh.at[place], h_send.at[n], h_recv.at[n], earlier) for n, place in enumerate((slot, facing))
    ]

    def h_start(n):
        @pl.when(has_earlier)
        def _():
            h_copies[n].start()

    def h_wait(n):
        @pl.when(has_later)
        def _():
            h_copies[n].wait_recv()

        @pl.when(jnp.logical_not(has_later))
        def _():
            for m in range(5):
                gh[(slot, facing)[n], m] = jnp.zeros((ROWS, LANES), bf16)


    def piece(ref, part, p):
        return ref.at[pl.ds(QUARTER * lax.rem(part + 4, 4) + PIECE * p, PIECE)]

    def t_copy(p):
        return copy(piece(t_hbm, y, p), piece(t_far, y, p), t_send.at[p], t_recv.at[p], mirror)

    def y_copy(p, n):
        block = piece(t_far, y, p)
        return copy(block, block, y_send.at[p, n], y_recv.at[p, n], column[n])

    def y_pass(p):
        t_copy(p).wait_recv()
        for n in (2, 0, 1):
            y_copy(p, n).start()

    def y_build(p):
        for n in range(3):
            part = y + (-1, 1, 2)[n]
            block = piece(t_far, part, p)
            copy(block, block, y_send.at[p, n], y_recv.at[p, n], column[n]).wait_recv()
            build_toeplitz(t_far, tz_far, wcol_far, QUARTER * lax.rem(part + 4, 4) + PIECE * p, PIECE)

    n_copy = copy(n_out, n_in, n_send, n_recv, mirror)
    r_copy = copy(r_out, r_in, r_send, r_recv, partner)

    for p in range(3):
        t_copy(p).start()
    h_start(0)
    for n in (2, 0, 1):
        x_copy(0, n).start()
    s_copy(0, 0).start()
    loads[1].wait()
    loads[2].wait()
    number_rows(idx_ref, mask_ref, zh, mine, theirs, mcol)
    flat = jnp.transpose(theirs[...])[0:8, :]
    sixteens = jnp.floor(flat * (1.0 / 16.0))
    n_out[...] = jnp.concatenate([sixteens, flat - 16.0 * sixteens], axis=0).astype(bf16)
    n_copy.start()
    choose(mine[0:TRACES, 0:1], ids, 0)
    loads[3].wait()
    build_toeplitz(t_ref, tz, wcol, 0, GROUPS)
    y_pass(0)
    h_wait(0)
    for n in range(2):
        x_copy(1, n).start()
    s_copy(1, 0).start()
    x_wait(0, 2)
    h_start(1)
    s_copy(0, 3).start()
    y_pass(1)
    y_pass(2)
    for n in range(2):
        x_wait(0, n)
        s_copy(0, 1 + n).start()
    build_toeplitz(t_far, tz_far, wcol_far, QUARTER * y, QUARTER)
    n_copy.wait_recv()
    got = n_in[...].astype(f32)
    choose(jnp.transpose(got[0:8] * 16.0 + got[8:16])[0:TRACES, 0:1], ids, TRACES)
    y_build(0)
    h_wait(1)
    s_copy(1, 3).start()
    for n in range(2):
        x_wait(1, n)
        s_copy(1, 1 + n).start()
    y_build(1)
    s_wait(0)
    xs[:, :TIME] = pick(ids[...], gm, 0, 5)
    band = band_matrix()
    y_build(2)
    s_wait(1)
    xs[pl.ds(TRACES, TRACES), TIME:] = pick(ids[pl.ds(TRACES, TRACES), :], gh, 0, 5)
    spread(xs, wb, TRACES)
    window_scales(xs, band, sc, TRACES)
    acc = jnp.zeros((96, LANES), f32)
    acc = correlate(tz_far, wb, sc, wcol_far, TRACES, 0, GROUPS, acc, 36)
    r_out[...] = fold(acc)

    @pl.when(first_half)
    def _():
        pl.semaphore_wait(meet, 1)

    r_copy.start()
    xs[pl.ds(0, TRACES), TIME:] = pick(ids[pl.ds(0, TRACES), :], gh, 0, 5)
    spread(xs, wb, 0)
    window_scales(xs, band, sc, 0)
    total = fold(correlate(tz, wb, sc, wcol, 0, 0, GROUPS, jnp.zeros((96, LANES), f32), 12))
    r_copy.wait_recv()
    sums[...] = total + r_in[...]
    finish(sums, mcol, o_ref)

    for p in range(3):
        t_copy(p).wait_send()
        for n in range(3):
            y_copy(p, n).wait_send()
    for n in range(3):
        x_copy(0, n).wait_send()
    for n in range(2):
        x_copy(1, n).wait_send()
    for n in range(4):
        for s in range(2):
            s_copy(s, n).wait_send()
    for sent in (n_copy, r_copy):
        sent.wait_send()

    @pl.when(has_earlier)
    def _():
        for h in h_copies:
            h.wait_send()


def per_device(waveform, templates, station_index, channel_mask):
    w = jnp.transpose(waveform, (1, 0, 2))
    t = jnp.transpose(templates, (1, 2, 0, 3)).reshape(GROUPS, MEMBERS, TPL)
    mask = jnp.transpose(channel_mask, (2, 0, 1))
    anywhere = pl.BlockSpec(memory_space=pl.ANY)
    dma = pltpu.SemaphoreType.DMA
    return pl.pallas_call(
        kernel,
        out_shape=jax.ShapeDtypeStruct((MEMBERS, TIME), f32),
        in_specs=[anywhere] * 4,
        out_specs=pl.BlockSpec(memory_space=pltpu.VMEM),
        scratch_shapes=[
            pltpu.VMEM(w.shape, bf16),
            pltpu.VMEM(t.shape, bf16),
            pltpu.SMEM(station_index.shape, i32),
            pltpu.SMEM(mask.shape, i32),
            pltpu.VMEM(t.shape, bf16),
            pltpu.VMEM((16, 256), bf16),
            pltpu.VMEM((16, 256), bf16),
            pltpu.VMEM((SLOTS, 5, ROWS, LANES), bf16),
            pltpu.VMEM((SLOTS, 5, ROWS, LANES), bf16),
            pltpu.VMEM((2 * TRACES, HALF), bf16),
            pltpu.VMEM((GROUPS, LANES, TIME), bf16),
            pltpu.VMEM((GROUPS, LANES, TIME), bf16),
            pltpu.VMEM((256, LANES), f32),
            pltpu.VMEM((256, LANES), f32),
            pltpu.VMEM((GROUPS, MEMBERS, LANES), f32),
            pltpu.VMEM((GROUPS, MEMBERS, LANES), f32),
            pltpu.VMEM((TRACES, LANES), f32),
            pltpu.VMEM((2 * TRACES, 2 * TIME), f32),
            pltpu.VMEM((2 * TRACES * 40, LANES), f32),
            pltpu.VMEM((2 * TRACES * 24, LANES), f32),
            pltpu.VMEM((24, LANES), f32),
            pltpu.VMEM((24, LANES), f32),
            pltpu.VMEM((24, LANES), f32),
            dma((4,)),
            dma((2, 3)),
            dma((2, 3)),
            dma((2, 4)),
            dma((2, 4)),
            dma((2,)),
            dma((2,)),
            dma((3,)),
            dma((3,)),
            dma((3, 3)),
            dma((3, 3)),
            dma,
            dma,
            dma,
            dma,
            pltpu.SemaphoreType.REGULAR,
        ],
        compiler_params=pltpu.CompilerParams(
            collective_id=0, has_side_effects=True, vmem_limit_bytes=56 * 2**20
        ),
    )(w, t, station_index, mask)


def solution(mesh):
    return jax.shard_map(
        per_device,
        mesh=mesh,
        in_specs=(
            P("blk", None, "tm"),
            P("blk", None, None, None),
            P("blk", None),
            P("blk", None, None),
        ),
        out_specs=P("blk", "tm"),
        check_vma=False,
    )
```

```python
import jax
import jax.numpy as jnp
from jax import lax
from jax.experimental import pallas as pl
from jax.experimental.pallas import tpu as pltpu
from jax.sharding import PartitionSpec as P

bf16, f32, i32 = jnp.bfloat16, jnp.float32, jnp.int32
MESH = pl.DeviceIdType.MESH
NT = (((1,), (1,)), ((), ()))

TPL = 600
TIME = 640
PER = 25
ROWS = 80
SUB = 32
LANES = 128
GROUPS = 36
MEMBERS = 4
TRACES = GROUPS * MEMBERS
HALF = 8 * ROWS
SLOTS = 8
QUARTER = GROUPS // 4
PIECE = QUARTER // 3


def build_toeplitz(t_ref, tz, wcol, first, count, step=3):
    def body(g, carry):
        group = first + step * g
        tt = t_ref[pl.ds(group, step)].astype(f32)
        norm = lax.rsqrt(jnp.sum(tt * tt, axis=2, keepdims=True) + 1e-6)
        wcol[pl.ds(group, step)] = jnp.broadcast_to(norm, (step, MEMBERS, LANES))
        padded = jnp.concatenate([tt, jnp.zeros((step, MEMBERS, TIME - TPL), f32)], axis=2)
        for i in range(step):
            for k in range(MEMBERS):
                rows = jnp.broadcast_to(padded[i, k : k + 1], (SUB, TIME))
                tz[group + i, pl.ds(SUB * k, SUB), :] = pltpu.roll(rows, 0, 1, stride=1, stride_axis=0).astype(bf16)
        return carry

    lax.fori_loop(0, count // step, body, 0)


def number_rows(idx_ref, mask_ref, zh, mine, theirs, mcol):
    def body(g, carry):
        row0 = pl.multiple_of(8 * g, 8)
        for i in range(8):
            jc = 2 * g + i // 4
            k = i % 4
            j = jc // 3
            c = jc - 3 * j
            station = idx_ref[k, j]
            used = mask_ref[c, k, j]
            owner = station // PER
            half = owner // 8
            row = ((owner - 8 * half) * ROWS + c * PER + (station - PER * owner) + 1) * used
            here = half * zh + (1 - half) * (1 - zh)
            mine[pl.ds(row0 + i, 1), :] = jnp.full((1, LANES), (row * here).astype(f32), f32)
            theirs[pl.ds(row0 + i, 1), :] = jnp.full((1, LANES), (row * (1 - here)).astype(f32), f32)
            mcol[pl.ds(row0 + i, 1), :] = jnp.full((1, LANES), used.astype(f32), f32)
        return carry

    lax.fori_loop(0, GROUPS // 2, body, 0)


def band_matrix():
    u = lax.broadcasted_iota(i32, (768, LANES), 0)
    b = lax.broadcasted_iota(i32, (768, LANES), 1)
    d = u - b
    return jnp.where((d >= 0) & (d < TPL), 1.0, 0.0).astype(bf16)


def choose(rows, ids, base):
    number = lax.broadcasted_iota(i32, (TRACES, HALF), 1).astype(f32) + 1.0
    ids[pl.ds(base, TRACES), :] = jnp.where(jnp.broadcast_to(rows, (TRACES, HALF)) == number, 1.0, 0.0).astype(bf16)


def pick(ids, store, first, count):
    blocks = [store[:, first + i].reshape(HALF, LANES) for i in range(count)]
    return jnp.dot(ids, jnp.concatenate(blocks, axis=1), preferred_element_type=f32)


def spread(xs, wb, base):
    full = xs[pl.ds(base, TRACES), :]
    for a in range(4):
        moved = full if a == 0 else pltpu.roll(full, 2 * TIME - SUB * a, 1)
        for m in range(10):
            wb[pl.ds(40 * base + 4 * m + a, TRACES, stride=40), :] = moved[:, LANES * m : LANES * (m + 1)]


def window_scales(xs, band, sc, base):
    high, low = [], []
    for m in range(10):
        part = xs[pl.ds(base, TRACES), LANES * m : LANES * (m + 1)]
        square = part * part
        top = square.astype(bf16)
        high.append(top)
        low.append((square - top.astype(f32)).astype(bf16))
    lane = lax.broadcasted_iota(i32, (TRACES, LANES), 1) // SUB
    member = lax.rem(lax.broadcasted_iota(i32, (TRACES, LANES), 0), MEMBERS)
    for a in range(5):
        energy = jnp.dot(jnp.concatenate(high[a : a + 6], axis=1), band, preferred_element_type=f32)
        energy += jnp.dot(jnp.concatenate(low[a : a + 6], axis=1), band, preferred_element_type=f32)
        scale = lax.rsqrt(jnp.maximum(energy, 0.25 * TPL))
        turned = [scale] + [pltpu.roll(scale, SUB * d, 1) for d in range(1, 4)]
        for a2 in range(4):
            v = jnp.zeros((TRACES, LANES), f32)
            for k in range(MEMBERS):
                v = jnp.where((lane == k) & (member == k), turned[(k - a2) % 4], v)
            sc[pl.ds(24 * base + 4 * a + a2, TRACES, stride=24), :] = v


def correlate(tz, wb, sc, wcol, base, first, count, acc, unroll=9):
    def body(g, acc):
        for q in range(unroll):
            jc = first + g * unroll + q
            parts, gains = [], []
            for k in range(MEMBERS):
                row = pl.multiple_of((base + jc * MEMBERS + k) * 40, 8)
                parts.append(jnp.concatenate([wb[pl.ds(row + 4 * p, 24), :] for p in range(5)], axis=1))
                gains.append(jnp.broadcast_to(wcol[jc, k : k + 1, :], (24, LANES)))
            windows = jnp.concatenate(parts, axis=0).astype(bf16)
            c = lax.dot_general(windows, tz[jc], NT, preferred_element_type=f32)
            scale = sc[pl.ds(pl.multiple_of((base + jc * MEMBERS) * 24, 8), 96), :]
            acc = acc + c * (scale * jnp.concatenate(gains, axis=0))
        return acc

    return lax.fori_loop(0, count // unroll, body, acc)


def fold(acc):
    return (acc[0:24] + acc[24:48]) + (acc[48:72] + acc[72:96])


def finish(sums, mcol, o_ref):
    counts = jnp.sum(mcol[...].reshape(GROUPS, MEMBERS, LANES), axis=0)
    factor = jnp.sqrt(TPL / counts)
    lane = lax.broadcasted_iota(i32, (8, LANES), 1) // SUB
    quads = [sums[pl.ds(q, 5, stride=4), :] for q in range(4)]
    quads = [jnp.concatenate([rows, jnp.zeros((3, LANES), f32)], axis=0) for rows in quads]
    for k in range(MEMBERS):
        out = jnp.zeros((8, LANES), f32)
        for q in range(4):
            rows = quads[q] if q == k else pltpu.roll(quads[q], (SUB * (q - k)) % LANES, 1)
            out = jnp.where(lane == q, rows, out)
        for m in range(5):
            o_ref[k : k + 1, LANES * m : LANES * (m + 1)] = out[m : m + 1, :] * factor[k : k + 1, :]


def kernel(
    w_hbm, t_hbm, idx_hbm, mask_hbm, o_ref,
    w_ref, t_ref, idx_ref, mask_ref, t_far, n_out, n_in, gm, gh, ids, tz, tz_far, mine, theirs, wcol, wcol_far, mcol,
    xs, wb, sc, r_out, r_in, sums,
    in_sem, x_send, x_recv, s_send, s_recv, h_send, h_recv, t_send, t_recv, y_send, y_recv, n_send, n_recv, r_send, r_recv, meet,
):
    blk, tm = lax.axis_index("blk"), lax.axis_index("tm")
    zh, x, core = blk // 8, lax.rem(blk // 2, 4), lax.rem(blk, 2)
    zl, y = tm // 4, lax.rem(tm, 4)

    def at(place, c):
        return lax.rem(place + 4, 4) * 2 + c

    loads = [
        pltpu.make_async_copy(src, dst, in_sem.at[i])
        for i, (src, dst) in enumerate(
            ((w_hbm, w_ref), (idx_hbm, idx_ref), (mask_hbm, mask_ref), (t_hbm, t_ref))
        )
    ]
    loads[0].start()

    other = (1 - zh) * 8 + at(x, core)
    partner = (other, tm)
    mirror = (other, (7 - zl) * 4 + y)
    sibling = (zh * 8 + at(x, 1 - core), tm)
    across = [(zh * 8 + at(x + d, core), tm) for d in (1, -1, 2)]
    column = [(blk, zl * 4 + lax.rem(y + d + 4, 4)) for d in (1, -1, 2)]
    earlier, later = (blk, lax.rem(tm + 31, 32)), (blk, lax.rem(tm + 1, 32))
    has_earlier, has_later = tm > 0, tm < 31

    barrier = pltpu.get_barrier_semaphore()
    friends = (mirror, *across, *column, sibling)
    for friend in friends:
        pl.semaphore_signal(barrier, inc=1, device_id=friend, device_id_type=MESH)

    first_half = zh == 0

    @pl.when(first_half)
    def _():
        pl.semaphore_signal(barrier, inc=1, device_id=partner, device_id_type=MESH)

    @pl.when(has_earlier)
    def _():
        pl.semaphore_signal(barrier, inc=1, device_id=earlier, device_id_type=MESH)

    @pl.when(has_later)
    def _():
        pl.semaphore_signal(barrier, inc=1, device_id=later, device_id_type=MESH)

    for load in loads[1:]:
        load.start()
    loads[0].wait()
    own = w_ref[...].astype(f32)
    packed = jnp.concatenate([own[0], own[1], own[2], jnp.zeros((ROWS - 3 * PER, TIME), f32)], axis=0)
    slot = at(x, core)
    for m in range(5):
        gm[slot, m] = packed[:, LANES * m : LANES * (m + 1)].astype(bf16)
    pl.semaphore_wait(barrier, len(friends) + zh + has_earlier.astype(i32) + has_later.astype(i32))

    @pl.when(jnp.logical_not(first_half))
    def _():
        pl.semaphore_signal(meet, inc=1, device_id=partner, device_id_type=MESH)

    def copy(src, dst, send, recv, to):
        return pltpu.make_async_remote_copy(
            src_ref=src, dst_ref=dst, send_sem=send, recv_sem=recv, device_id=to, device_id_type=MESH
        )

    store = (gm, gh)

    def x_copy(s, n):
        block = store[s].at[slot]
        return copy(block, block, x_send.at[s, n], x_recv.at[s, n], across[n])

    def x_wait(s, n):
        block = store[s].at[at(x + (-1, 1, 2)[n], core)]
        copy(block, block, x_send.at[s, n], x_recv.at[s, n], across[n]).wait_recv()

    def s_copy(s, n):
        block = store[s].at[at(x + (0, -1, 1, 2)[n], core)]
        return copy(block, block, s_send.at[s, n], s_recv.at[s, n], sibling)

    def s_wait(s):
        for n in range(4):
            block = store[s].at[at(x + (0, -1, 1, 2)[n], 1 - core)]
            copy(block, block, s_send.at[s, n], s_recv.at[s, n], sibling).wait_recv()

    facing = at(x + 2, core)
    h_copies = [
        copy(gm.at[place], gh.at[place], h_send.at[n], h_recv.at[n], earlier) for n, place in enumerate((slot, facing))
    ]

    def h_start(n):
        @pl.when(has_earlier)
        def _():
            h_copies[n].start()

    def h_wait(n):
        @pl.when(has_later)
        def _():
            h_copies[n].wait_recv()

        @pl.when(jnp.logical_not(has_later))
        def _():
            for m in range(5):
                gh[(slot, facing)[n], m] = jnp.zeros((ROWS, LANES), bf16)


    def piece(ref, part, p):
        return ref.at[pl.ds(QUARTER * lax.rem(part + 4, 4) + PIECE * p, PIECE)]

    def t_copy(p):
        return copy(piece(t_hbm, y, p), piece(t_far, y, p), t_send.at[p], t_recv.at[p], mirror)

    def y_copy(p, n):
        block = piece(t_far, y, p)
        return copy(block, block, y_send.at[p, n], y_recv.at[p, n], column[n])

    def y_pass(p):
        t_copy(p).wait_recv()
        for n in (2, 0, 1):
            y_copy(p, n).start()

    def y_build(p):
        for n in range(3):
            part = y + (-1, 1, 2)[n]
            block = piece(t_far, part, p)
            copy(block, block, y_send.at[p, n], y_recv.at[p, n], column[n]).wait_recv()
            build_toeplitz(t_far, tz_far, wcol_far, QUARTER * lax.rem(part + 4, 4) + PIECE * p, PIECE)

    n_copy = copy(n_out, n_in, n_send, n_recv, mirror)
    r_copy = copy(r_out, r_in, r_send, r_recv, partner)

    for p in range(3):
        t_copy(p).start()
    h_start(0)
    for n in (2, 0, 1):
        x_copy(0, n).start()
    s_copy(0, 0).start()
    loads[1].wait()
    loads[2].wait()
    number_rows(idx_ref, mask_ref, zh, mine, theirs, mcol)
    flat = jnp.transpose(theirs[...])[0:8, :]
    sixteens = jnp.floor(flat * (1.0 / 16.0))
    n_out[...] = jnp.concatenate([sixteens, flat - 16.0 * sixteens], axis=0).astype(bf16)
    n_copy.start()
    choose(mine[0:TRACES, 0:1], ids, 0)
    loads[3].wait()
    build_toeplitz(t_ref, tz, wcol, 0, GROUPS)
    y_pass(0)
    h_wait(0)
    for n in range(2):
        x_copy(1, n).start()
    s_copy(1, 0).start()
    x_wait(0, 2)
    h_start(1)
    s_copy(0, 3).start()
    y_pass(1)
    y_pass(2)
    for n in range(2):
        x_wait(0, n)
        s_copy(0, 1 + n).start()
    build_toeplitz(t_far, tz_far, wcol_far, QUARTER * y, QUARTER)
    n_copy.wait_recv()
    got = n_in[...].astype(f32)
    choose(jnp.transpose(got[0:8] * 16.0 + got[8:16])[0:TRACES, 0:1], ids, TRACES)
    y_build(0)
    h_wait(1)
    s_copy(1, 3).start()
    for n in range(2):
        x_wait(1, n)
        s_copy(1, 1 + n).start()
    y_build(1)
    s_wait(0)
    xs[:, :TIME] = pick(ids[...], gm, 0, 5)
    band = band_matrix()
    y_build(2)
    s_wait(1)
    xs[pl.ds(TRACES, TRACES), TIME:] = pick(ids[pl.ds(TRACES, TRACES), :], gh, 0, 5)
    spread(xs, wb, TRACES)
    window_scales(xs, band, sc, TRACES)
    acc = jnp.zeros((96, LANES), f32)
    acc = correlate(tz_far, wb, sc, wcol_far, TRACES, 0, GROUPS, acc, 36)
    r_out[...] = fold(acc)

    @pl.when(first_half)
    def _():
        pl.semaphore_wait(meet, 1)

    r_copy.start()
    xs[pl.ds(0, TRACES), TIME:] = pick(ids[pl.ds(0, TRACES), :], gh, 0, 5)
    spread(xs, wb, 0)
    window_scales(xs, band, sc, 0)
    total = fold(correlate(tz, wb, sc, wcol, 0, 0, GROUPS, jnp.zeros((96, LANES), f32), 36))
    r_copy.wait_recv()
    sums[...] = total + r_in[...]
    finish(sums, mcol, o_ref)

    for p in range(3):
        t_copy(p).wait_send()
        for n in range(3):
            y_copy(p, n).wait_send()
    for n in range(3):
        x_copy(0, n).wait_send()
    for n in range(2):
        x_copy(1, n).wait_send()
    for n in range(4):
        for s in range(2):
            s_copy(s, n).wait_send()
    for sent in (n_copy, r_copy):
        sent.wait_send()

    @pl.when(has_earlier)
    def _():
        for h in h_copies:
            h.wait_send()


def per_device(waveform, templates, station_index, channel_mask):
    w = jnp.transpose(waveform, (1, 0, 2))
    t = jnp.transpose(templates, (1, 2, 0, 3)).reshape(GROUPS, MEMBERS, TPL)
    mask = jnp.transpose(channel_mask, (2, 0, 1))
    anywhere = pl.BlockSpec(memory_space=pl.ANY)
    dma = pltpu.SemaphoreType.DMA
    return pl.pallas_call(
        kernel,
        out_shape=jax.ShapeDtypeStruct((MEMBERS, TIME), f32),
        in_specs=[anywhere] * 4,
        out_specs=pl.BlockSpec(memory_space=pltpu.VMEM),
        scratch_shapes=[
            pltpu.VMEM(w.shape, bf16),
            pltpu.VMEM(t.shape, bf16),
            pltpu.SMEM(station_index.shape, i32),
            pltpu.SMEM(mask.shape, i32),
            pltpu.VMEM(t.shape, bf16),
            pltpu.VMEM((16, 256), bf16),
            pltpu.VMEM((16, 256), bf16),
            pltpu.VMEM((SLOTS, 5, ROWS, LANES), bf16),
            pltpu.VMEM((SLOTS, 5, ROWS, LANES), bf16),
            pltpu.VMEM((2 * TRACES, HALF), bf16),
            pltpu.VMEM((GROUPS, LANES, TIME), bf16),
            pltpu.VMEM((GROUPS, LANES, TIME), bf16),
            pltpu.VMEM((256, LANES), f32),
            pltpu.VMEM((256, LANES), f32),
            pltpu.VMEM((GROUPS, MEMBERS, LANES), f32),
            pltpu.VMEM((GROUPS, MEMBERS, LANES), f32),
            pltpu.VMEM((TRACES, LANES), f32),
            pltpu.VMEM((2 * TRACES, 2 * TIME), f32),
            pltpu.VMEM((2 * TRACES * 40, LANES), f32),
            pltpu.VMEM((2 * TRACES * 24, LANES), f32),
            pltpu.VMEM((24, LANES), f32),
            pltpu.VMEM((24, LANES), f32),
            pltpu.VMEM((24, LANES), f32),
            dma((4,)),
            dma((2, 3)),
            dma((2, 3)),
            dma((2, 4)),
            dma((2, 4)),
            dma((2,)),
            dma((2,)),
            dma((3,)),
            dma((3,)),
            dma((3, 3)),
            dma((3, 3)),
            dma,
            dma,
            dma,
            dma,
            pltpu.SemaphoreType.REGULAR,
        ],
        compiler_params=pltpu.CompilerParams(
            collective_id=0, has_side_effects=True, vmem_limit_bytes=56 * 2**20
        ),
    )(w, t, station_index, mask)


def solution(mesh):
    return jax.shard_map(
        per_device,
        mesh=mesh,
        in_specs=(
            P("blk", None, "tm"),
            P("blk", None, None, None),
            P("blk", None),
            P("blk", None, None),
        ),
        out_specs=P("blk", "tm"),
        check_vma=False,
    )
```
